256 devices in a mesh: gx: 4 (over x), wa: 64 (over y, z, core).
Axes of the slice: x: 4, y: 4, z: 8, core: 2. Of those that a mesh axis runs over, the one named last changes fastest.
Arguments:
- mixing_ratio: float32 [1536, 48, 1536], P('wa', 'gx'), may hold values from 0 to 1
- thermal_state: float32 [1536, 48, 1536], P('wa', 'gx'), may hold values from 1 to 3
- streamwise_speed: float32 [1536, 1536], P('wa'), may hold values from 0.5 to 2
- implicit_derivative_matrix: bfloat16 [1536, 1536], replicated, may hold values from -0.15625 to 0.15625
- stored_entry_slices: bfloat16 [2, 1536, 8, 1536], P(None, 'wa', 'gx'), may hold values from 0 to 2
- orifice_region_flag: int32 [1536, 1536], P('wa'), may hold values 0 or 1
- arriving_slice_number: int32 [1], replicated, may hold values from 0 to 7
- joint_frequency_class: int32 [1536, 48, 12], P('wa', 'gx'), may hold values from 0 to 4095
Outputs:
- mixture_next: float32 [1536, 48, 1536], P('wa', 'gx')
- temperature_next: float32 [1536, 48, 1536], P('wa', 'gx')
- histogram: float32 [64, 64], replicated
The draws below stay inside these ranges and needn't reach their ends.
All inputs are finite; a program needn't handle non-finite values. No bound on the sum of `orifice_region_flag` on one device may be relied on, other than what follows from the above.
Results may differ from the reference program's by a relative error of at most 0.00057.
Values may be sent and summed in bfloat16 or wider, within the bound.
No kernel may reach another device: no remote copies, remote signals or barrier semaphores. Data moves between devices by JAX's collectives and lax.ppermute only.
A program may use at most 128 MiB of HBM per device.

```python
import jax
import jax.numpy as jnp
from jax import lax

LATERAL_EXTENT_A = 1536
LATERAL_EXTENT_B = 1536
PX_DEV = 12
HB = 64
ZBLK = 128
STREAMWISE_COUNT = 48
DBP = 8
CELLS_PER_BIN = 27648


def place_ends(drawn, rng, low, top_value):
    place = [jax.random.randint(jax.random.fold_in(rng, axis), (), 0, length) for axis, length in enumerate(drawn.shape)]
    main_axis = drawn.shape.index(max(drawn.shape))
    neighbour = place[:main_axis] + [(place[main_axis] + 1) % drawn.shape[main_axis]] + place[main_axis + 1:]
    return drawn.at[tuple(place)].set(low).at[tuple(neighbour)].set(top_value)


def block_scale(key, extent, pieces, least, largest):
    loudness = 1.0
    for dim, parts in pieces:
        draws = jax.random.uniform(jax.random.fold_in(jax.random.fold_in(key, 6), dim), (parts,), jnp.float32, least / len(pieces), largest / len(pieces))
        loudness = loudness * jnp.repeat(jnp.exp(draws), extent[dim] // parts).reshape((-1,) + (1,) * (len(extent) - 1 - dim))
    return loudness


def gaussian(key, extent, spread, reach, kind=jnp.bfloat16):
    values = jax.random.normal(key, extent, jnp.float32) * spread
    return jnp.minimum(jnp.maximum(values, -reach), reach).astype(kind)


def setup_inputs(seed: int = 0) -> dict:
    arg_keys = jax.random.split(jax.random.key(seed), 9)
    return {
        "mixing_ratio": jnp.clip(1.0 * jax.random.uniform(arg_keys[0], (LATERAL_EXTENT_A, STREAMWISE_COUNT, LATERAL_EXTENT_B), jnp.float32) ** block_scale(arg_keys[0], (LATERAL_EXTENT_A, STREAMWISE_COUNT, LATERAL_EXTENT_B), ((0, 64), (1, 4)), -0.2, 0.2), 0.0, 1.0),
        "thermal_state": jnp.clip(1.0 + 2.0 * jax.random.uniform(arg_keys[1], (LATERAL_EXTENT_A, STREAMWISE_COUNT, LATERAL_EXTENT_B), jnp.float32) ** block_scale(arg_keys[1], (LATERAL_EXTENT_A, STREAMWISE_COUNT, LATERAL_EXTENT_B), ((0, 64), (1, 4)), -0.2, 0.2), 1.0, 3.0),
        "streamwise_speed": jnp.clip(0.5 + 1.5 * jax.random.uniform(arg_keys[2], (LATERAL_EXTENT_A, LATERAL_EXTENT_B), jnp.float32) ** block_scale(arg_keys[2], (LATERAL_EXTENT_A, LATERAL_EXTENT_B), ((0, 64),), -0.2, 0.2), 0.5, 2.0),
        "implicit_derivative_matrix": gaussian(arg_keys[3], (LATERAL_EXTENT_A, LATERAL_EXTENT_A), LATERAL_EXTENT_A ** -0.5, 0.15625),
        "stored_entry_slices": jnp.clip(2.0 * jax.random.uniform(arg_keys[4], (2, LATERAL_EXTENT_A, DBP, LATERAL_EXTENT_B), jnp.float32) ** block_scale(arg_keys[4], (2, LATERAL_EXTENT_A, DBP, LATERAL_EXTENT_B), ((1, 64), (2, 4)), -0.2, 0.2), 0.0, 2.0).astype(jnp.bfloat16),
        "orifice_region_flag": place_ends((jax.random.randint(arg_keys[5], (LATERAL_EXTENT_A, LATERAL_EXTENT_B), 0, 3) < 1).astype(jnp.int32), jax.random.fold_in(arg_keys[5], 1), 0, 1),
        "arriving_slice_number": jax.random.randint(arg_keys[6], (1,), 0, DBP).astype(jnp.int32),
        "joint_frequency_class": place_ends(jax.random.randint(arg_keys[7], (LATERAL_EXTENT_A, STREAMWISE_COUNT, LATERAL_EXTENT_B // ZBLK), 0, HB * HB), jax.random.fold_in(arg_keys[7], 1), 0, (HB * HB) - 1).astype(jnp.int32),
    }


mixing_diffusivity = 0.3
heat_diffusivity = 0.4
release_rate = 0.5
phase_step = 0.2


def reference(mixing_ratio, thermal_state, streamwise_speed, implicit_derivative_matrix, stored_entry_slices, orifice_region_flag, arriving_slice_number, joint_frequency_class):
    transported_quantities = jnp.stack([mixing_ratio, thermal_state])
    plane_index = arriving_slice_number[0].astype(jnp.int32)
    database_plane = lax.dynamic_index_in_dim(stored_entry_slices, plane_index, 2, keepdims=False).astype(jnp.float32)
    coflow = jnp.array([0.0, 1.0], jnp.float32)[:, None, None]
    inflow_cells = jnp.where(orifice_region_flag[None] == 1, database_plane, coflow)
    extended = jnp.concatenate([inflow_cells[:, :, None], transported_quantities, transported_quantities[:, :, -1:]], axis=2)
    diffusivity = jnp.array([mixing_diffusivity, heat_diffusivity], jnp.float32)[:, None, None]

    def plane_update(slab_index):
        upstream = lax.dynamic_index_in_dim(extended, slab_index, 2, keepdims=False)
        current = lax.dynamic_index_in_dim(extended, slab_index + 1, 2, keepdims=False)
        downstream = lax.dynamic_index_in_dim(extended, slab_index + 2, 2, keepdims=False)
        rounded = current.astype(jnp.bfloat16)
        depth_slope = jnp.einsum("fyj,kj->fyk", rounded, implicit_derivative_matrix, preferred_element_type=jnp.float32).astype(jnp.bfloat16)
        depth_curve = jnp.einsum("fyj,kj->fyk", depth_slope, implicit_derivative_matrix, preferred_element_type=jnp.float32)
        radial_slope = jnp.einsum("ij,fjz->fiz", implicit_derivative_matrix, rounded, preferred_element_type=jnp.float32).astype(jnp.bfloat16)
        radial_curve = jnp.einsum("ij,fjz->fiz", implicit_derivative_matrix, radial_slope, preferred_element_type=jnp.float32).astype(jnp.bfloat16)
        axial_slope = (downstream - upstream) * 0.5
        axial_curve = downstream - 2.0 * current + upstream
        radial_float = radial_slope.astype(jnp.float32)
        depth_float = depth_slope.astype(jnp.float32)
        dissipation = 2.0 * mixing_diffusivity * (axial_slope[0] ** 2 + radial_float[0] ** 2 + depth_float[0] ** 2)
        laplace = axial_curve + radial_curve.astype(jnp.float32) + depth_curve
        release = jnp.stack([jnp.zeros_like(dissipation), release_rate * dissipation])
        fringe = 1.0 / (1.0 + slab_index.astype(jnp.float32) / PX_DEV)
        rhs = -streamwise_speed[None] * axial_slope + diffusivity * laplace + release + fringe * (inflow_cells - current)
        updated = current + phase_step * rhs
        block_sums = dissipation.reshape(LATERAL_EXTENT_A, LATERAL_EXTENT_B // ZBLK, ZBLK).sum(axis=-1)
        return updated, block_sums

    updated, block_sums = lax.map(plane_update, jnp.arange(STREAMWISE_COUNT, dtype=jnp.int32))
    updated = jnp.transpose(updated, (1, 2, 0, 3))
    block_sums = jnp.transpose(block_sums, (1, 0, 2))
    histogram = jax.ops.segment_sum(block_sums.reshape(-1), joint_frequency_class.reshape(-1), num_segments=HB * HB)
    histogram = (histogram / CELLS_PER_BIN).reshape(HB, HB)
    return updated[0], updated[1], histogram
```

```python
import functools

import jax
import jax.numpy as jnp
from jax import lax
from jax.experimental import pallas as pl
from jax.experimental.pallas import tpu as pltpu
from jax.sharding import PartitionSpec as P

HB = 64
ZBLK = 128
LANES = 128
ROWS = 8

mixing_diffusivity = 0.3
heat_diffusivity = 0.4
release_rate = 0.5
phase_step = 0.2

VMEM_LIMIT = 56 * 1024 * 1024


def lane_group(shape):
    return lax.broadcasted_iota(jnp.int32, shape, len(shape) - 1) // 32


def blocks(planes, depth):
    per_plane = depth // ZBLK
    for block in range(planes * per_plane):
        yield block, block // per_plane, (block % per_plane) * ZBLK


def pack_kernel(x_ref, spare_ref, out_ref):
    planes, _, depth = x_ref.shape
    whole = 2 * out_ref.shape[0]
    group = lane_group((ROWS, LANES))
    for block, p, k in blocks(planes, depth):
        tiles = [x_ref[p, ROWS * t : ROWS * t + ROWS, k : k + ZBLK] for t in range(3)]
        if block < whole:
            for t in range(3):
                out_ref[block // 2, 3 * (block % 2) + t] = tiles[t].astype(jnp.bfloat16)
            continue
        for q in range(4):
            line = 4 * (block - whole) + q
            packed = spare_ref[line] if spare_ref is not None else jnp.zeros_like(tiles[0])
            for g in range(3):
                shift = (32 * (g - q)) % LANES
                moved = pltpu.roll(tiles[g], shift, 1) if shift else tiles[g]
                packed = jnp.where(group == g, moved, packed)
            out_ref[line, 6] = packed.astype(jnp.bfloat16)


def pack(x, lines, spare=None):
    body = pack_kernel if spare is not None else lambda x_ref, out_ref: pack_kernel(x_ref, None, out_ref)
    operands = (x,) if spare is None else (x, spare)
    return pl.pallas_call(
        body,
        out_shape=jax.ShapeDtypeStruct((lines, 7, ROWS, LANES), jnp.bfloat16),
        compiler_params=pltpu.CompilerParams(vmem_limit_bytes=VMEM_LIMIT),
        cost_estimate=pl.CostEstimate(flops=x.size, bytes_accessed=6 * x.size, transcendentals=0),
        name="pack",
    )(*operands)


def unpack_add_kernel(scale, part_ref, ret_ref, out_ref):
    planes, _, depth = part_ref.shape
    whole = 2 * ret_ref.shape[0]
    group = lane_group((ROWS, LANES))
    for block, p, k in blocks(planes, depth):
        if block < whole:
            tiles = [ret_ref[block // 2, 3 * (block % 2) + t].astype(jnp.float32) for t in range(3)]
        else:
            quarters = [ret_ref[4 * (block - whole) + q, 6].astype(jnp.float32) for q in range(4)]
            tiles = []
            for g in range(3):
                tile = None
                for q in range(4):
                    shift = (32 * (q - g)) % LANES
                    moved = pltpu.roll(quarters[q], shift, 1) if shift else quarters[q]
                    tile = moved if tile is None else jnp.where(group == q, moved, tile)
                tiles.append(tile)
        for t in range(3):
            at = (p, slice(ROWS * t, ROWS * t + ROWS), slice(k, k + ZBLK))
            out_ref[at] = part_ref[at] + scale * tiles[t]


def unpack_add(part, ret, scale):
    return pl.pallas_call(
        functools.partial(unpack_add_kernel, scale),
        out_shape=jax.ShapeDtypeStruct(part.shape, jnp.float32),
        compiler_params=pltpu.CompilerParams(vmem_limit_bytes=VMEM_LIMIT),
        cost_estimate=pl.CostEstimate(flops=2 * part.size, bytes_accessed=10 * part.size, transcendentals=0),
        name="unpack_add",
    )(part, ret)


SOURCES = 16


def unpack_lines(r_ref, x_ref):
    def step(i, carry):
        src = pl.ds(i * SOURCES, SOURCES)
        rows = pl.ds(pl.multiple_of(i * (24 * SOURCES), 24 * SOURCES), 24 * SOURCES)
        for b in range(2):
            tiles = r_ref[src, 3 * b : 3 * b + 3].astype(jnp.float32)
            x_ref[rows, b * LANES : (b + 1) * LANES] = tiles.reshape(24 * SOURCES, LANES).astype(jnp.bfloat16)
        last = r_ref[src, 6].astype(jnp.float32).reshape(ROWS * SOURCES, LANES)
        parts = [last] + [pltpu.roll(last, LANES - 32 * g, 1) for g in (1, 2)]
        tiles = jnp.stack([part.reshape(SOURCES, ROWS, LANES) for part in parts], axis=1)
        x_ref[rows, 2 * LANES : 3 * LANES] = tiles.reshape(24 * SOURCES, LANES).astype(jnp.bfloat16)
        return carry

    lax.fori_loop(0, r_ref.shape[0] // SOURCES, step, 0)


def pack_lines(values, out_ref, i):
    src = pl.ds(i * SOURCES, SOURCES)
    for b in range(2):
        tiles = values[:, b * LANES : (b + 1) * LANES].reshape(SOURCES, 3, ROWS, LANES)
        out_ref[src, 3 * b : 3 * b + 3] = tiles.astype(jnp.bfloat16)
    tiles = values[:, 2 * LANES :].reshape(SOURCES, 3, ROWS, LANES)
    group = lane_group((ROWS * SOURCES, LANES))
    packed = jnp.zeros((ROWS * SOURCES, LANES), jnp.float32)
    for g in range(3):
        tile = tiles[:, g].reshape(ROWS * SOURCES, LANES)
        packed = jnp.where(group == g, pltpu.roll(tile, 32 * g, 1) if g else tile, packed)
    out_ref[src, 6] = packed.reshape(SOURCES, ROWS, LANES).astype(jnp.bfloat16)


def line_kernel(heat, *refs):
    if heat:
        r_ref, d_ref, mixture_slope_ref, out_ref, x_ref, slope_ref = refs
    else:
        r_ref, d_ref, out_ref, slope_ref, sums_ref, x_ref = refs
    unpack_lines(r_ref, x_ref)
    tile = 24 * SOURCES
    count = r_ref.shape[0] // SOURCES

    def slope_step(i, carry):
        rows = pl.ds(pl.multiple_of(i * tile, tile), tile)
        slope = jnp.dot(d_ref[rows, :], x_ref[...], preferred_element_type=jnp.float32).astype(jnp.bfloat16)
        slope_ref[rows, :] = slope
        if not heat:
            squared = slope.astype(jnp.float32) ** 2
            lane = lax.broadcasted_iota(jnp.int32, (tile, LANES), 1)
            sums = jnp.zeros((tile, LANES), jnp.float32)
            for b in range(3):
                part = squared[:, b * LANES : (b + 1) * LANES]
                if b == 2:
                    part = jnp.where(lane < 32, part, 0.0)
                sums = jnp.where(lane == b, jnp.sum(part, axis=1, keepdims=True), sums)
            sums_ref[rows, :] = sums
        return carry

    lax.fori_loop(0, count, slope_step, 0)

    def curve_step(i, carry):
        rows = pl.ds(pl.multiple_of(i * tile, tile), tile)
        curve = jnp.dot(d_ref[rows, :], slope_ref[...], preferred_element_type=jnp.float32)
        if heat:
            slope = mixture_slope_ref[rows, :].astype(jnp.float32)
            curve = heat_diffusivity * curve + (release_rate * 2.0 * mixing_diffusivity) * slope**2
        pack_lines(curve, out_ref, i)
        return carry

    lax.fori_loop(0, count, curve_step, 0)


def line_call(received, matrix, mixture_slope=None):
    heat = mixture_slope is not None
    rows = matrix.shape[0]
    packet = jax.ShapeDtypeStruct(received.shape, jnp.bfloat16)
    wide = (rows, 3 * LANES)
    if heat:
        out_shape = packet
        scratch = [pltpu.VMEM(wide, jnp.bfloat16), pltpu.VMEM(wide, jnp.bfloat16)]
        operands = (received, matrix, mixture_slope)
    else:
        out_shape = (
            packet,
            jax.ShapeDtypeStruct(wide, jnp.bfloat16),
            jax.ShapeDtypeStruct((rows, LANES), jnp.float32),
        )
        scratch = [pltpu.VMEM(wide, jnp.bfloat16)]
        operands = (received, matrix)
    return pl.pallas_call(
        functools.partial(line_kernel, heat),
        out_shape=out_shape,
        scratch_shapes=scratch,
        compiler_params=pltpu.CompilerParams(vmem_limit_bytes=VMEM_LIMIT),
        cost_estimate=pl.CostEstimate(
            flops=4 * rows * rows * 3 * LANES, bytes_accessed=2 * rows * rows + 8 * rows * LANES, transcendentals=0
        ),
        name="heat_lines" if heat else "mixture_lines",
    )(*operands)


def local_kernel(
    fringe_ref, lo_ref, hi_ref, *refs
):
    fields = (refs[0:3], refs[3:6])
    slope_ref, curve_ref, speed_ref, inflow_ref, mix_ref, heat_ref, sums_ref = refs[6:]
    p = pl.program_id(0)
    last = pl.num_programs(0) - 1
    fringe = fringe_ref[p]
    speed = speed_ref[...]
    dissipation = None
    for f, (before, here, after) in enumerate(fields):
        x = here[0]
        upstream = jnp.where(p == 0, lo_ref[f], before[0])
        downstream = jnp.where(p == last, hi_ref[f], after[0])
        axial_slope = (downstream - upstream) * 0.5
        axial_curve = downstream - 2.0 * x + upstream
        diffusivity = (mixing_diffusivity, heat_diffusivity)[f]
        rhs = -speed * axial_slope + diffusivity * (axial_curve + curve_ref[f, 0]) + fringe * (inflow_ref[f] - x)
        if f == 0:
            depth = slope_ref[0, 0].astype(jnp.float32)
            dissipation = (2.0 * mixing_diffusivity) * (axial_slope**2 + depth**2)
            mix_ref[0] = x + phase_step * rhs
        else:
            heat_ref[0] = x + phase_step * (rhs + release_rate * dissipation)
    lane = lax.broadcasted_iota(jnp.int32, sums_ref.shape[1:], 1)
    sums = jnp.zeros(sums_ref.shape[1:], jnp.float32)
    for k in range(dissipation.shape[1] // ZBLK):
        part = jnp.sum(dissipation[:, k * ZBLK : (k + 1) * ZBLK], axis=1, keepdims=True)
        sums = jnp.where(lane == k, part, sums)
    sums_ref[0] = sums


def local_terms(x0, x1, lo, hi, slope, curve, speed, inflow, fringe):
    planes, rows, depth = x0.shape
    plane = lambda move: pl.BlockSpec((1, rows, depth), lambda p: (jnp.clip(p + move, 0, planes - 1), 0, 0))
    fixed = lambda shape: pl.BlockSpec(shape, lambda p: (0,) * len(shape))
    return pl.pallas_call(
        local_kernel,
        grid=(planes,),
        in_specs=[
            pl.BlockSpec(memory_space=pltpu.SMEM),
            fixed((2, rows, depth)),
            fixed((2, rows, depth)),
            plane(-1),
            plane(0),
            plane(1),
            plane(-1),
            plane(0),
            plane(1),
            pl.BlockSpec((1, 1, rows, depth), lambda p: (0, p, 0, 0)),
            pl.BlockSpec((2, 1, rows, depth), lambda p: (0, p, 0, 0)),
            fixed((rows, depth)),
            fixed((2, rows, depth)),
        ],
        out_specs=[
            pl.BlockSpec((1, rows, depth), lambda p: (p, 0, 0)),
            pl.BlockSpec((1, rows, depth), lambda p: (p, 0, 0)),
            pl.BlockSpec((1, rows, LANES), lambda p: (p, 0, 0)),
        ],
        out_shape=[
            jax.ShapeDtypeStruct((planes, rows, depth), jnp.float32),
            jax.ShapeDtypeStruct((planes, rows, depth), jnp.float32),
            jax.ShapeDtypeStruct((planes, rows, LANES), jnp.float32),
        ],
        compiler_params=pltpu.CompilerParams(vmem_limit_bytes=VMEM_LIMIT),
        cost_estimate=pl.CostEstimate(flops=60 * x0.size, bytes_accessed=34 * x0.size, transcendentals=0),
        name="local_terms",
    )(fringe, lo, hi, x0, x0, x0, x1, x1, x1, slope, curve, speed, inflow)


def bin_sums(values, classes):
    row = classes // HB
    column = classes % HB
    bins = jnp.arange(HB, dtype=jnp.int32)[:, None]
    columns = (bins == column[None]).astype(jnp.bfloat16)
    total = 0.0
    for _ in range(3):
        term = values.astype(jnp.bfloat16)
        values = values - term.astype(jnp.float32)
        rows = jnp.where(bins == row[None], term[None], jnp.zeros((), jnp.bfloat16))
        total = total + jnp.einsum("rn,cn->rc", rows, columns, preferred_element_type=jnp.float32)
    return total


def all_sum(block):
    for axis in ("wa", "gx"):
        count = lax.axis_size(axis)
        step = 1
        while step < count:
            block = block + lax.ppermute(block, axis, [(i, i ^ step) for i in range(count)])
            step *= 2
    return block


def body(
    mixing_ratio,
    thermal_state,
    streamwise_speed,
    implicit_derivative_matrix,
    stored_entry_slices,
    orifice_region_flag,
    arriving_slice_number,
    joint_frequency_class,
):
    matrix = implicit_derivative_matrix
    row_count, plane_count, depth_count = mixing_ratio.shape
    lines = lax.axis_size("wa")
    slab_index = lax.axis_index("gx")
    slab_count = lax.axis_size("gx")
    x0 = jnp.transpose(mixing_ratio, (1, 0, 2))
    x1 = jnp.transpose(thermal_state, (1, 0, 2))

    def exchange(packets):
        return lax.all_to_all(packets, "wa", split_axis=0, concat_axis=0, tiled=True)

    classes = joint_frequency_class.reshape(3, ROWS, plane_count * depth_count // ZBLK)
    whole = classes[:, :, : 2 * lines].reshape(3, ROWS, lines, 2)
    quarter = jnp.repeat(classes[:, :, 2 * lines :], 4, axis=2)[..., None]
    sent_classes = jnp.concatenate([whole, quarter], axis=3).transpose(2, 1, 0, 3).reshape(lines, ROWS, 9)
    spare = jnp.concatenate([sent_classes // HB, sent_classes % HB], axis=2).astype(jnp.float32)
    spare = jnp.pad(spare, ((0, 0), (0, 0), (96, LANES - 96 - 18)))

    lines0 = exchange(pack(x0, lines))
    lines1 = exchange(pack(x1, lines, spare))

    held_count = stored_entry_slices.shape[2]
    plane_index = arriving_slice_number[0]
    owner = plane_index // held_count
    held_plane = lax.dynamic_index_in_dim(stored_entry_slices, plane_index % held_count, 2, keepdims=False)
    database_plane = held_plane
    for move in range(1, slab_count):
        table = [(i, (i + move) % slab_count) for i in range(slab_count)]
        arrived = lax.ppermute(held_plane, "gx", table)
        database_plane = jnp.where((slab_index - move) % slab_count == owner, arrived, database_plane)
    forward = [(i, i + 1) for i in range(slab_count - 1)]
    backward = [(target, source) for source, target in forward]
    first = jnp.stack([x0[0], x1[0]])
    final = jnp.stack([x0[-1], x1[-1]])
    before = lax.ppermute(final.astype(jnp.bfloat16), "gx", forward).astype(jnp.float32)
    after = lax.ppermute(first.astype(jnp.bfloat16), "gx", backward).astype(jnp.float32)
    coflow = jnp.array([0.0, 1.0], jnp.float32)[:, None, None]
    inflow_cells = jnp.where(orifice_region_flag[None] == 1, database_plane.astype(jnp.float32), coflow)
    lo = jnp.where(slab_index == 0, inflow_cells, before)
    hi = jnp.where(slab_index == slab_count - 1, final, after)

    rounded = jnp.stack([x0, x1]).astype(jnp.bfloat16)
    depth_slope = jnp.einsum(
        "fxyj,kj->fxyk", rounded, matrix, preferred_element_type=jnp.float32
    ).astype(jnp.bfloat16)
    depth_curve = jnp.einsum("fxyj,kj->fxyk", depth_slope, matrix, preferred_element_type=jnp.float32)
    plane_numbers = (slab_index * plane_count + jnp.arange(plane_count, dtype=jnp.int32)).astype(jnp.float32)
    fringe = 1.0 / (1.0 + plane_numbers / plane_count)
    part0, part1, local_sums = local_terms(
        x0, x1, lo, hi, depth_slope, depth_curve, streamwise_speed, inflow_cells, fringe
    )

    returned0, mixture_slope, line_sums = line_call(lines0, matrix)
    back0 = exchange(returned0)
    returned1 = line_call(lines1, matrix, mixture_slope)
    back1 = exchange(returned1)

    per_plane = depth_count // ZBLK
    own_values = local_sums[:, :, :per_plane].reshape(-1)
    own_classes = joint_frequency_class.transpose(1, 0, 2).reshape(-1)
    line_values = (2.0 * mixing_diffusivity) * line_sums.reshape(lines, 3, ROWS, LANES)[..., :3].reshape(-1)
    codes = lines1[:, 6, :, 96:114].astype(jnp.int32).reshape(lines, ROWS, 2, 3, 3)
    line_classes = (codes[:, :, 0] * HB + codes[:, :, 1]).transpose(0, 2, 1, 3).reshape(-1)
    bins = bin_sums(
        jnp.concatenate([own_values, line_values]), jnp.concatenate([own_classes, line_classes])
    )
    summed = all_sum(bins)
    per_bin = row_count * lines * plane_count * slab_count * depth_count // (HB * HB)
    histogram = summed / per_bin

    mixture_next = unpack_add(part0, back0, phase_step * mixing_diffusivity)
    temperature_next = unpack_add(part1, back1, phase_step)
    return (jnp.transpose(mixture_next, (1, 0, 2)), jnp.transpose(temperature_next, (1, 0, 2)), histogram)


def solution(mesh):
    in_specs = (
        P("wa", "gx", None),
        P("wa", "gx", None),
        P("wa", None),
        P(),
        P(None, "wa", "gx", None),
        P("wa", None),
        P(),
        P("wa", "gx", None),
    )
    out_specs = (P("wa", "gx", None), P("wa", "gx", None), P())
    return jax.shard_map(body, mesh=mesh, in_specs=in_specs, out_specs=out_specs, check_vma=False)
```

```python
import functools

import jax
import jax.numpy as jnp
from jax import lax
from jax.experimental import pallas as pl
from jax.experimental.pallas import tpu as pltpu
from jax.sharding import PartitionSpec as P

HB = 64
ZBLK = 128
LANES = 128
ROWS = 8

mixing_diffusivity = 0.3
heat_diffusivity = 0.4
release_rate = 0.5
phase_step = 0.2

VMEM_LIMIT = 56 * 1024 * 1024
LOCAL_VMEM_LIMIT = 16 * 1024 * 1024
LINE_VMEM_LIMIT = 40 * 1024 * 1024


PACK_PLANES = 2


def lane_group(shape):
    return lax.broadcasted_iota(jnp.int32, shape, len(shape) - 1) // 32


def rolled(tile, shift):
    shift = shift % LANES
    return pltpu.roll(tile, shift, 1) if shift else tile


def pack_kernel(x0_ref, x1_ref, class_ref, out_ref, wide_ref, high_ref, low_ref):
    step = pl.program_id(0)
    steps = pl.num_programs(0)
    lines = out_ref.shape[0]
    per_plane = x0_ref.shape[2] // ZBLK
    pairs = per_plane // 2
    left = per_plane * PACK_PLANES - (2 * lines - per_plane * PACK_PLANES * (steps - 1))
    first_left = per_plane * PACK_PLANES - left
    group = lane_group((ROWS, LANES))
    sublane = lax.broadcasted_iota(jnp.int32, (ROWS, LANES), 0)
    spare = (lax.broadcasted_iota(jnp.int32, (ROWS, LANES), 1) < 120) & (group == 3)

    def copy_pairs(count):
        for pair in range(count):
            p, k = pair // pairs, (pair % pairs) * 2 * ZBLK
            line = step * (PACK_PLANES * pairs) + pair
            for f, x_ref in enumerate((x0_ref, x1_ref)):
                for b in range(2):
                    for t in range(3):
                        tile = x_ref[p, ROWS * t : ROWS * t + ROWS, k + b * ZBLK : k + (b + 1) * ZBLK]
                        out_ref[line, 7 * f + 3 * b + t] = tile.astype(jnp.bfloat16)

    @pl.when(step == 0)
    def _():
        wide_ref[...] = jnp.zeros_like(wide_ref)
        for p in range(class_ref.shape[0]):
            wide_ref[p, :per_plane, : class_ref.shape[2]] = class_ref[p]
        for p in range(class_ref.shape[0]):
            codes = pltpu.roll(wide_ref[p], 96, 1)
            high = codes // HB
            high_ref[p] = high.astype(jnp.float32)
            low_ref[p] = (codes - HB * high).astype(jnp.float32)

    @pl.when(step < steps - 1)
    def _():
        copy_pairs(PACK_PLANES * pairs)

    @pl.when(step == steps - 1)
    def _():
        copy_pairs(first_left // 2)
        for m in range(left):
            block = first_left + m
            p, k = block // per_plane, (block % per_plane) * ZBLK
            plane, row = class_ref.shape[0] - PACK_PLANES + p, block % per_plane
            for q in range(4):
                line = 4 * m + q
                places = [(2 * line // per_plane, 2 * line % per_plane), (2 * line // per_plane, 2 * line % per_plane + 1)]
                places.append((plane, row))
                classes = jnp.zeros((ROWS, LANES), jnp.float32)
                for at, ref in ((0, high_ref), (3, low_ref)):
                    for b, (cp, cr) in enumerate(places):
                        classes = jnp.where(sublane == at + b, ref[cp, cr : cr + 1, :], classes)
                classes = jnp.where(spare, classes, 0.0)
                for f, x_ref in enumerate((x0_ref, x1_ref)):
                    packed = classes if f == 0 else jnp.zeros_like(classes)
                    for g in range(3):
                        tile = x_ref[p, ROWS * g : ROWS * g + ROWS, k : k + ZBLK]
                        packed = jnp.where(group == g, rolled(tile, 32 * (g - q)), packed)
                    out_ref[line, 7 * f + 6] = packed.astype(jnp.bfloat16)


def pack(x0, x1, classes, lines):
    planes, rows, depth = x0.shape
    part = pl.BlockSpec((PACK_PLANES, rows, depth), lambda i: (i, 0, 0))
    packets = (lines, 14, ROWS, LANES)
    wide = (planes, 2 * ROWS, LANES)
    return pl.pallas_call(
        pack_kernel,
        grid=(planes // PACK_PLANES,),
        in_specs=[part, part, pl.BlockSpec(classes.shape, lambda i: (0, 0, 0))],
        out_specs=pl.BlockSpec(packets, lambda i: (0, 0, 0, 0)),
        out_shape=jax.ShapeDtypeStruct(packets, jnp.bfloat16),
        scratch_shapes=[
            pltpu.VMEM(wide, jnp.int32),
            pltpu.VMEM(wide, jnp.float32),
            pltpu.VMEM(wide, jnp.float32),
        ],
        compiler_params=pltpu.CompilerParams(vmem_limit_bytes=VMEM_LIMIT),
        cost_estimate=pl.CostEstimate(flops=2 * x0.size, bytes_accessed=12 * x0.size, transcendentals=0),
        name="pack",
    )(x0, x1, classes)


def unpack_add_kernel(part0_ref, part1_ref, ret_ref, out0_ref, out1_ref):
    step = pl.program_id(0)
    steps = pl.num_programs(0)
    lines = ret_ref.shape[0]
    per_plane = part0_ref.shape[2] // ZBLK
    pairs = per_plane // 2
    left = per_plane * PACK_PLANES - (2 * lines - per_plane * PACK_PLANES * (steps - 1))
    first_left = per_plane * PACK_PLANES - left
    group = lane_group((ROWS, LANES))
    fields = (
        (part0_ref, out0_ref, phase_step * mixing_diffusivity),
        (part1_ref, out1_ref, phase_step),
    )

    def add_pairs(count):
        for pair in range(count):
            p, k = pair // pairs, (pair % pairs) * 2 * ZBLK
            line = step * (PACK_PLANES * pairs) + pair
            for f, (part_ref, out_ref, scale) in enumerate(fields):
                for b in range(2):
                    for t in range(3):
                        at = (p, slice(ROWS * t, ROWS * t + ROWS), slice(k + b * ZBLK, k + (b + 1) * ZBLK))
                        tile = ret_ref[line, 7 * f + 3 * b + t].astype(jnp.float32)
                        out_ref[at] = part_ref[at] + scale * tile

    @pl.when(step < steps - 1)
    def _():
        add_pairs(PACK_PLANES * pairs)

    @pl.when(step == steps - 1)
    def _():
        add_pairs(first_left // 2)
        for m in range(left):
            block = first_left + m
            p, k = block // per_plane, (block % per_plane) * ZBLK
            for f, (part_ref, out_ref, scale) in enumerate(fields):
                quarters = [ret_ref[4 * m + q, 7 * f + 6].astype(jnp.float32) for q in range(4)]
                for g in range(3):
                    tile = rolled(quarters[0], -32 * g)
                    for q in range(1, 4):
                        tile = jnp.where(group == q, rolled(quarters[q], 32 * (q - g)), tile)
                    at = (p, slice(ROWS * g, ROWS * g + ROWS), slice(k, k + ZBLK))
                    out_ref[at] = part_ref[at] + scale * tile


def unpack_add(part0, part1, returned):
    planes, rows, depth = part0.shape
    part = pl.BlockSpec((PACK_PLANES, rows, depth), lambda i: (i, 0, 0))
    return pl.pallas_call(
        unpack_add_kernel,
        grid=(planes // PACK_PLANES,),
        in_specs=[part, part, pl.BlockSpec(returned.shape, lambda i: (0, 0, 0, 0))],
        out_specs=[part, part],
        out_shape=[jax.ShapeDtypeStruct(part0.shape, jnp.float32)] * 2,
        compiler_params=pltpu.CompilerParams(vmem_limit_bytes=VMEM_LIMIT),
        cost_estimate=pl.CostEstimate(flops=4 * part0.size, bytes_accessed=20 * part0.size, transcendentals=0),
        name="unpack_add",
    )(part0, part1, returned)


SOURCES = 16
WIDE = 2 * LANES
MATMUL_ROWS = 768


def unpack_lines(r_ref, x_ref):
    def step(i, carry):
        src = pl.ds(i * SOURCES, SOURCES)
        rows = pl.ds(pl.multiple_of(i * (24 * SOURCES), 24 * SOURCES), 24 * SOURCES)
        for f in range(2):
            for b in range(2):
                tiles = r_ref[src, 7 * f + 3 * b : 7 * f + 3 * b + 3].astype(jnp.float32)
                x_ref[f, rows, b * LANES : (b + 1) * LANES] = tiles.reshape(24 * SOURCES, LANES).astype(jnp.bfloat16)
            last = r_ref[src, 7 * f + 6].astype(jnp.float32).reshape(ROWS * SOURCES, LANES)
            parts = [rolled(last, -32 * g).reshape(SOURCES, ROWS, LANES) for g in range(3)]
            tiles = jnp.stack(parts, axis=1)
            x_ref[2, rows, f * LANES : (f + 1) * LANES] = tiles.reshape(24 * SOURCES, LANES).astype(jnp.bfloat16)
        return carry

    lax.fori_loop(0, r_ref.shape[0] // SOURCES, step, 0)


def pack_whole(values, out_ref, src, f):
    for b in range(2):
        tiles = values[:, b * LANES : (b + 1) * LANES].reshape(-1, 3, ROWS, LANES)
        out_ref[src, 7 * f + 3 * b : 7 * f + 3 * b + 3] = tiles.astype(jnp.bfloat16)


def pack_quarter(values, out_ref, src, f):
    tiles = values.reshape(-1, 3, ROWS, LANES)
    group = lane_group((tiles.shape[0] * ROWS, LANES))
    packed = jnp.zeros(group.shape, jnp.float32)
    for g in range(3):
        packed = jnp.where(group == g, rolled(tiles[:, g].reshape(group.shape), 32 * g), packed)
    out_ref[src, 7 * f + 6] = packed.reshape(-1, ROWS, LANES).astype(jnp.bfloat16)


def line_kernel(r_ref, d_ref, out_ref, sums_ref, x_ref, slope_ref):
    unpack_lines(r_ref, x_ref)
    tile = MATMUL_ROWS
    count = d_ref.shape[0] // tile

    def slope_step(i, carry):
        rows = pl.ds(pl.multiple_of(i * tile, tile), tile)
        lane = lax.broadcasted_iota(jnp.int32, (tile, LANES), 1)
        sums = jnp.zeros((tile, LANES), jnp.float32)
        for n in range(3):
            slope = jnp.dot(d_ref[rows, :], x_ref[n], preferred_element_type=jnp.float32).astype(jnp.bfloat16)
            slope_ref[n, rows, :] = slope
            if n == 1:
                continue
            for b in range(2) if n == 0 else range(1):
                part = slope[:, b * LANES : (b + 1) * LANES].astype(jnp.float32) ** 2
                if n == 2:
                    part = jnp.where(lane < 32, part, 0.0)
                sums = jnp.where(lane == n + b, jnp.sum(part, axis=1, keepdims=True), sums)
        sums_ref[rows, :] = sums
        return carry

    lax.fori_loop(0, count, slope_step, 0)

    def curve_step(i, carry):
        rows = pl.ds(pl.multiple_of(i * tile, tile), tile)
        src = pl.ds(i * (tile // 24), tile // 24)
        matrix = d_ref[rows, :]

        def heat(curve, slope):
            slope = slope.astype(jnp.float32)
            return heat_diffusivity * curve + (release_rate * 2.0 * mixing_diffusivity) * slope**2

        pack_whole(jnp.dot(matrix, slope_ref[0], preferred_element_type=jnp.float32), out_ref, src, 0)
        curve = jnp.dot(matrix, slope_ref[1], preferred_element_type=jnp.float32)
        pack_whole(heat(curve, slope_ref[0, rows, :]), out_ref, src, 1)
        curve = jnp.dot(matrix, slope_ref[2], preferred_element_type=jnp.float32)
        pack_quarter(curve[:, :LANES], out_ref, src, 0)
        pack_quarter(heat(curve[:, LANES:], slope_ref[2, rows, :LANES]), out_ref, src, 1)
        return carry

    lax.fori_loop(0, count, curve_step, 0)


def line_terms(received, matrix):
    rows = matrix.shape[0]
    wide = (3, rows, WIDE)
    return pl.pallas_call(
        line_kernel,
        out_shape=(
            jax.ShapeDtypeStruct(received.shape, jnp.bfloat16),
            jax.ShapeDtypeStruct((rows, LANES), jnp.float32),
        ),
        scratch_shapes=[pltpu.VMEM(wide, jnp.bfloat16), pltpu.VMEM(wide, jnp.bfloat16)],
        compiler_params=pltpu.CompilerParams(vmem_limit_bytes=LINE_VMEM_LIMIT),
        cost_estimate=pl.CostEstimate(
            flops=12 * rows * rows * WIDE, bytes_accessed=2 * rows * rows + 4 * received.size, transcendentals=0
        ),
        name="line_terms",
    )(received, matrix)


def local_kernel(
    fringe_ref, lo_ref, hi_ref, *refs
):
    fields = (refs[0:3], refs[3:6])
    slope_ref, curve_ref, speed_ref, inflow_ref, mix_ref, heat_ref, sums_ref = refs[6:]
    p = pl.program_id(0)
    last = pl.num_programs(0) - 1
    fringe = fringe_ref[p]
    speed = speed_ref[...]
    dissipation = None
    for f, (before, here, after) in enumerate(fields):
        x = here[0]
        upstream = jnp.where(p == 0, lo_ref[f], before[0])
        downstream = jnp.where(p == last, hi_ref[f], after[0])
        axial_slope = (downstream - upstream) * 0.5
        axial_curve = downstream - 2.0 * x + upstream
        diffusivity = (mixing_diffusivity, heat_diffusivity)[f]
        rhs = -speed * axial_slope + diffusivity * (axial_curve + curve_ref[f, 0]) + fringe * (inflow_ref[f] - x)
        if f == 0:
            depth = slope_ref[0, 0].astype(jnp.float32)
            dissipation = (2.0 * mixing_diffusivity) * (axial_slope**2 + depth**2)
            mix_ref[0] = x + phase_step * rhs
        else:
            heat_ref[0] = x + phase_step * (rhs + release_rate * dissipation)
    lane = lax.broadcasted_iota(jnp.int32, sums_ref.shape[1:], 1)
    sums = jnp.zeros(sums_ref.shape[1:], jnp.float32)
    for k in range(dissipation.shape[1] // ZBLK):
        part = jnp.sum(dissipation[:, k * ZBLK : (k + 1) * ZBLK], axis=1, keepdims=True)
        sums = jnp.where(lane == k, part, sums)
    sums_ref[0] = sums


def local_terms(x0, x1, lo, hi, slope, curve, speed, inflow, fringe):
    planes, rows, depth = x0.shape
    plane = lambda move: pl.BlockSpec((1, rows, depth), lambda p: (jnp.clip(p + move, 0, planes - 1), 0, 0))
    fixed = lambda shape: pl.BlockSpec(shape, lambda p: (0,) * len(shape))
    return pl.pallas_call(
        local_kernel,
        grid=(planes,),
        in_specs=[
            pl.BlockSpec(memory_space=pltpu.SMEM),
            fixed((2, rows, depth)),
            fixed((2, rows, depth)),
            plane(-1),
            plane(0),
            plane(1),
            plane(-1),
            plane(0),
            plane(1),
            pl.BlockSpec((1, 1, rows, depth), lambda p: (0, p, 0, 0)),
            pl.BlockSpec((2, 1, rows, depth), lambda p: (0, p, 0, 0)),
            fixed((rows, depth)),
            fixed((2, rows, depth)),
        ],
        out_specs=[
            pl.BlockSpec((1, rows, depth), lambda p: (p, 0, 0)),
            pl.BlockSpec((1, rows, depth), lambda p: (p, 0, 0)),
            pl.BlockSpec((1, rows, LANES), lambda p: (p, 0, 0)),
        ],
        out_shape=[
            jax.ShapeDtypeStruct((planes, rows, depth), jnp.float32),
            jax.ShapeDtypeStruct((planes, rows, depth), jnp.float32),
            jax.ShapeDtypeStruct((planes, rows, LANES), jnp.float32),
        ],
        compiler_params=pltpu.CompilerParams(vmem_limit_bytes=LOCAL_VMEM_LIMIT),
        cost_estimate=pl.CostEstimate(flops=60 * x0.size, bytes_accessed=34 * x0.size, transcendentals=0),
        name="local_terms",
    )(fringe, lo, hi, x0, x0, x0, x1, x1, x1, slope, curve, speed, inflow)


def bin_sums(values, classes):
    row = classes // HB
    column = classes % HB
    bins = jnp.arange(HB, dtype=jnp.int32)[:, None]
    columns = (bins == column[None]).astype(jnp.bfloat16)
    total = 0.0
    for _ in range(3):
        term = values.astype(jnp.bfloat16)
        values = values - term.astype(jnp.float32)
        rows = jnp.where(bins == row[None], term[None], jnp.zeros((), jnp.bfloat16))
        total = total + jnp.einsum("rn,cn->rc", rows, columns, preferred_element_type=jnp.float32)
    return total


def all_sum(block):
    for axis, bits in (("gx", (1, 2)), ("wa", (1,)), ("wa", (16, 32)), ("wa", (2, 4)), ("wa", (8,))):
        count = lax.axis_size(axis)
        moves = bits if len(bits) == 1 else (bits[0], bits[1], bits[0] + bits[1])
        arrived = [lax.ppermute(block, axis, [(i, i ^ move) for i in range(count)]) for move in moves]
        block = block + arrived[0]
        if len(arrived) == 3:
            block = block + (arrived[1] + arrived[2])
    return block


def body(
    mixing_ratio,
    thermal_state,
    streamwise_speed,
    implicit_derivative_matrix,
    stored_entry_slices,
    orifice_region_flag,
    arriving_slice_number,
    joint_frequency_class,
):
    matrix = implicit_derivative_matrix
    row_count, plane_count, depth_count = mixing_ratio.shape
    lines = lax.axis_size("wa")
    slab_index = lax.axis_index("gx")
    slab_count = lax.axis_size("gx")
    x0 = jnp.transpose(mixing_ratio, (1, 0, 2))
    x1 = jnp.transpose(thermal_state, (1, 0, 2))

    def exchange(packets):
        return lax.all_to_all(packets, "wa", split_axis=0, concat_axis=0, tiled=True)

    classes = jnp.transpose(joint_frequency_class, (1, 2, 0))
    packets = pack(x0, x1, classes, lines)
    packets, x0, x1 = lax.optimization_barrier((packets, x0, x1))
    received = exchange(packets)

    rounded = jnp.stack([x0, x1]).astype(jnp.bfloat16)
    depth_slope = jnp.einsum(
        "fxyj,kj->fxyk", rounded, matrix, preferred_element_type=jnp.float32
    ).astype(jnp.bfloat16)
    depth_slope, stored_entry_slices, x0, x1 = lax.optimization_barrier((depth_slope, stored_entry_slices, x0, x1))

    held_count = stored_entry_slices.shape[2]
    plane_index = arriving_slice_number[0]
    owner = plane_index // held_count
    held_plane = lax.dynamic_index_in_dim(stored_entry_slices, plane_index % held_count, 2, keepdims=False)
    database_plane = held_plane
    for move in range(1, slab_count):
        table = [(i, (i + move) % slab_count) for i in range(slab_count)]
        arrived = lax.ppermute(held_plane, "gx", table)
        database_plane = jnp.where((slab_index - move) % slab_count == owner, arrived, database_plane)
    forward = [(i, i + 1) for i in range(slab_count - 1)]
    backward = [(target, source) for source, target in forward]
    first = jnp.stack([x0[0], x1[0]])
    final = jnp.stack([x0[-1], x1[-1]])
    before = lax.ppermute(final.astype(jnp.bfloat16), "gx", forward).astype(jnp.float32)
    after = lax.ppermute(first.astype(jnp.bfloat16), "gx", backward).astype(jnp.float32)
    coflow = jnp.array([0.0, 1.0], jnp.float32)[:, None, None]
    inflow_cells = jnp.where(orifice_region_flag[None] == 1, database_plane.astype(jnp.float32), coflow)
    lo = jnp.where(slab_index == 0, inflow_cells, before)
    hi = jnp.where(slab_index == slab_count - 1, final, after)

    depth_curve = jnp.einsum("fxyj,kj->fxyk", depth_slope, matrix, preferred_element_type=jnp.float32)
    plane_numbers = (slab_index * plane_count + jnp.arange(plane_count, dtype=jnp.int32)).astype(jnp.float32)
    fringe = 1.0 / (1.0 + plane_numbers / plane_count)
    part0, part1, local_sums = local_terms(
        x0, x1, lo, hi, depth_slope, depth_curve, streamwise_speed, inflow_cells, fringe
    )

    received, part0, part1, local_sums = lax.optimization_barrier((received, part0, part1, local_sums))
    returned, line_sums = line_terms(received, matrix)
    back = exchange(returned)

    per_plane = depth_count // ZBLK
    own_values = local_sums[:, :, :per_plane].transpose(0, 2, 1).reshape(-1)
    own_classes = classes.reshape(-1)
    line_values = (2.0 * mixing_diffusivity) * line_sums.reshape(lines, row_count, LANES)[..., :3]
    line_values = line_values.transpose(0, 2, 1).reshape(-1)
    codes = received[:, 6, :6, 96:120].astype(jnp.int32).reshape(lines, 2, 3, row_count)
    line_classes = (codes[:, 0] * HB + codes[:, 1]).reshape(-1)
    bins = bin_sums(
        jnp.concatenate([own_values, line_values]), jnp.concatenate([own_classes, line_classes])
    )
    summed = all_sum(bins)
    per_bin = row_count * lines * plane_count * slab_count * depth_count // (HB * HB)
    histogram = summed / per_bin

    mixture_next, temperature_next = unpack_add(part0, part1, back)
    return (jnp.transpose(mixture_next, (1, 0, 2)), jnp.transpose(temperature_next, (1, 0, 2)), histogram)


def solution(mesh):
    in_specs = (
        P("wa", "gx", None),
        P("wa", "gx", None),
        P("wa", None),
        P(),
        P(None, "wa", "gx", None),
        P("wa", None),
        P(),
        P("wa", "gx", None),
    )
    out_specs = (P("wa", "gx", None), P("wa", "gx", None), P())
    return jax.shard_map(body, mesh=mesh, in_specs=in_specs, out_specs=out_specs, check_vma=False)
```

```python
import functools

import jax
import jax.numpy as jnp
from jax import lax
from jax.experimental import pallas as pl
from jax.experimental.pallas import tpu as pltpu
from jax.sharding import PartitionSpec as P

HB = 64
ZBLK = 128
LANES = 128
ROWS = 8

mixing_diffusivity = 0.3
heat_diffusivity = 0.4
release_rate = 0.5
phase_step = 0.2

VMEM_LIMIT = 56 * 1024 * 1024
LOCAL_VMEM_LIMIT = 16 * 1024 * 1024
LINE_VMEM_LIMIT = 56 * 1024 * 1024
UNPACK_VMEM_LIMIT = 50 * 1024 * 1024


PACK_PLANES = 6


def lane_group(shape):
    return lax.broadcasted_iota(jnp.int32, shape, len(shape) - 1) // 32


def rolled(tile, shift):
    shift = shift % LANES
    return pltpu.roll(tile, shift, 1) if shift else tile


def pack_kernel(x0_ref, x1_ref, class_ref, out_ref, wide_ref, high_ref, low_ref):
    step = pl.program_id(0)
    steps = pl.num_programs(0)
    lines = out_ref.shape[0]
    per_plane = x0_ref.shape[2] // ZBLK
    pairs = per_plane // 2
    left = per_plane * PACK_PLANES - (2 * lines - per_plane * PACK_PLANES * (steps - 1))
    first_left = per_plane * PACK_PLANES - left
    group = lane_group((ROWS, LANES))
    sublane = lax.broadcasted_iota(jnp.int32, (ROWS, LANES), 0)
    spare = (lax.broadcasted_iota(jnp.int32, (ROWS, LANES), 1) < 120) & (group == 3)

    def copy_pairs(count):
        for pair in range(count):
            p, k = pair // pairs, (pair % pairs) * 2 * ZBLK
            line = step * (PACK_PLANES * pairs) + pair
            for f, x_ref in enumerate((x0_ref, x1_ref)):
                for b in range(2):
                    for t in range(3):
                        tile = x_ref[p, ROWS * t : ROWS * t + ROWS, k + b * ZBLK : k + (b + 1) * ZBLK]
                        out_ref[line, 7 * f + 3 * b + t] = tile.astype(jnp.bfloat16)

    @pl.when(step == 0)
    def _():
        wide_ref[...] = jnp.zeros_like(wide_ref)
        for p in range(class_ref.shape[0]):
            wide_ref[p, :per_plane, : class_ref.shape[2]] = class_ref[p]
        for p in range(class_ref.shape[0]):
            codes = pltpu.roll(wide_ref[p], 96, 1)
            high = codes // HB
            high_ref[p] = high.astype(jnp.float32)
            low_ref[p] = (codes - HB * high).astype(jnp.float32)

    @pl.when(step < steps - 1)
    def _():
        copy_pairs(PACK_PLANES * pairs)

    @pl.when(step == steps - 1)
    def _():
        copy_pairs(first_left // 2)
        for m in range(left):
            block = first_left + m
            p, k = block // per_plane, (block % per_plane) * ZBLK
            plane, row = class_ref.shape[0] - PACK_PLANES + p, block % per_plane
            for q in range(4):
                line = 4 * m + q
                places = [(2 * line // per_plane, 2 * line % per_plane), (2 * line // per_plane, 2 * line % per_plane + 1)]
                places.append((plane, row))
                classes = jnp.zeros((ROWS, LANES), jnp.float32)
                for at, ref in ((0, high_ref), (3, low_ref)):
                    for b, (cp, cr) in enumerate(places):
                        classes = jnp.where(sublane == at + b, ref[cp, cr : cr + 1, :], classes)
                classes = jnp.where(spare, classes, 0.0)
                for f, x_ref in enumerate((x0_ref, x1_ref)):
                    packed = classes if f == 0 else jnp.zeros_like(classes)
                    for g in range(3):
                        tile = x_ref[p, ROWS * g : ROWS * g + ROWS, k : k + ZBLK]
                        packed = jnp.where(group == g, rolled(tile, 32 * (g - q)), packed)
                    out_ref[line, 7 * f + 6] = packed.astype(jnp.bfloat16)


def pack(x0, x1, classes, lines):
    planes, rows, depth = x0.shape
    part = pl.BlockSpec((PACK_PLANES, rows, depth), lambda i: (i, 0, 0))
    packets = (lines, 14, ROWS, LANES)
    wide = (planes, 2 * ROWS, LANES)
    return pl.pallas_call(
        pack_kernel,
        grid=(planes // PACK_PLANES,),
        in_specs=[part, part, pl.BlockSpec(classes.shape, lambda i: (0, 0, 0))],
        out_specs=pl.BlockSpec(packets, lambda i: (0, 0, 0, 0)),
        out_shape=jax.ShapeDtypeStruct(packets, jnp.bfloat16),
        scratch_shapes=[
            pltpu.VMEM(wide, jnp.int32),
            pltpu.VMEM(wide, jnp.float32),
            pltpu.VMEM(wide, jnp.float32),
        ],
        compiler_params=pltpu.CompilerParams(vmem_limit_bytes=VMEM_LIMIT),
        cost_estimate=pl.CostEstimate(flops=2 * x0.size, bytes_accessed=12 * x0.size, transcendentals=0),
        name="pack",
    )(x0, x1, classes)


def unpack_add_kernel(parts_ref, ret_ref, out0_ref, out1_ref):
    step = pl.program_id(0)
    steps = pl.num_programs(0)
    lines = ret_ref.shape[0]
    per_plane = parts_ref.shape[3] // ZBLK
    pairs = per_plane // 2
    left = per_plane * PACK_PLANES - (2 * lines - per_plane * PACK_PLANES * (steps - 1))
    first_left = per_plane * PACK_PLANES - left
    group = lane_group((ROWS, LANES))
    fields = (
        (out0_ref, phase_step * mixing_diffusivity),
        (out1_ref, phase_step),
    )

    def add_pairs(count):
        for pair in range(count):
            p, k = pair // pairs, (pair % pairs) * 2 * ZBLK
            line = step * (PACK_PLANES * pairs) + pair
            for f, (out_ref, scale) in enumerate(fields):
                for b in range(2):
                    for t in range(3):
                        at = (p, slice(ROWS * t, ROWS * t + ROWS), slice(k + b * ZBLK, k + (b + 1) * ZBLK))
                        tile = ret_ref[line, 7 * f + 3 * b + t].astype(jnp.float32)
                        out_ref[at] = parts_ref[(f, *at)] + scale * tile

    @pl.when(step < steps - 1)
    def _():
        add_pairs(PACK_PLANES * pairs)

    @pl.when(step == steps - 1)
    def _():
        add_pairs(first_left // 2)
        for m in range(left):
            block = first_left + m
            p, k = block // per_plane, (block % per_plane) * ZBLK
            for f, (out_ref, scale) in enumerate(fields):
                quarters = [ret_ref[4 * m + q, 7 * f + 6].astype(jnp.float32) for q in range(4)]
                for g in range(3):
                    tile = rolled(quarters[0], -32 * g)
                    for q in range(1, 4):
                        tile = jnp.where(group == q, rolled(quarters[q], 32 * (q - g)), tile)
                    at = (p, slice(ROWS * g, ROWS * g + ROWS), slice(k, k + ZBLK))
                    out_ref[at] = parts_ref[(f, *at)] + scale * tile


def unpack_add(parts, returned):
    _, planes, rows, depth = parts.shape
    part = pl.BlockSpec((PACK_PLANES, rows, depth), lambda i: (i, 0, 0))
    return pl.pallas_call(
        unpack_add_kernel,
        grid=(planes // PACK_PLANES,),
        in_specs=[
            pl.BlockSpec((2, PACK_PLANES, rows, depth), lambda i: (0, i, 0, 0)),
            pl.BlockSpec(returned.shape, lambda i: (0, 0, 0, 0)),
        ],
        out_specs=[part, part],
        out_shape=[jax.ShapeDtypeStruct(parts.shape[1:], jnp.float32)] * 2,
        compiler_params=pltpu.CompilerParams(vmem_limit_bytes=UNPACK_VMEM_LIMIT),
        cost_estimate=pl.CostEstimate(flops=2 * parts.size, bytes_accessed=10 * parts.size, transcendentals=0),
        name="unpack_add",
    )(parts, returned)


SOURCES = 16
WIDE = 2 * LANES
MATMUL_ROWS = 1536


def unpack_lines(r_ref, x_ref):
    def step(i, carry):
        src = pl.ds(i * SOURCES, SOURCES)
        rows = pl.ds(pl.multiple_of(i * (24 * SOURCES), 24 * SOURCES), 24 * SOURCES)
        for f in range(2):
            for b in range(2):
                tiles = r_ref[src, 7 * f + 3 * b : 7 * f + 3 * b + 3].astype(jnp.float32)
                x_ref[f, rows, b * LANES : (b + 1) * LANES] = tiles.reshape(24 * SOURCES, LANES).astype(jnp.bfloat16)
            last = r_ref[src, 7 * f + 6].astype(jnp.float32).reshape(ROWS * SOURCES, LANES)
            parts = [rolled(last, -32 * g).reshape(SOURCES, ROWS, LANES) for g in range(3)]
            tiles = jnp.stack(parts, axis=1)
            x_ref[2, rows, f * LANES : (f + 1) * LANES] = tiles.reshape(24 * SOURCES, LANES).astype(jnp.bfloat16)
        return carry

    lax.fori_loop(0, r_ref.shape[0] // SOURCES, step, 0)


def pack_whole(values, out_ref, src, f):
    for b in range(2):
        tiles = values[:, b * LANES : (b + 1) * LANES].reshape(-1, 3, ROWS, LANES)
        out_ref[src, 7 * f + 3 * b : 7 * f + 3 * b + 3] = tiles.astype(jnp.bfloat16)


def pack_quarter(values, out_ref, src, f):
    tiles = values.reshape(-1, 3, ROWS, LANES)
    group = lane_group((tiles.shape[0] * ROWS, LANES))
    packed = jnp.zeros(group.shape, jnp.float32)
    for g in range(3):
        packed = jnp.where(group == g, rolled(tiles[:, g].reshape(group.shape), 32 * g), packed)
    out_ref[src, 7 * f + 6] = packed.reshape(-1, ROWS, LANES).astype(jnp.bfloat16)


def line_kernel(r_ref, matrix_ref, out_ref, sums_ref, x_ref, slope_ref, d_ref, arrived):
    copy = pltpu.make_async_copy(matrix_ref, d_ref, arrived)
    copy.start()
    unpack_lines(r_ref, x_ref)
    copy.wait()
    tile = MATMUL_ROWS
    count = d_ref.shape[0] // tile

    def slope_step(i, carry):
        rows = pl.ds(pl.multiple_of(i * tile, tile), tile)
        lane = lax.broadcasted_iota(jnp.int32, (tile, LANES), 1)
        sums = jnp.zeros((tile, LANES), jnp.float32)
        for n in range(3):
            slope = jnp.dot(d_ref[rows, :], x_ref[n], preferred_element_type=jnp.float32).astype(jnp.bfloat16)
            slope_ref[n, rows, :] = slope
            if n == 1:
                continue
            for b in range(2) if n == 0 else range(1):
                part = slope[:, b * LANES : (b + 1) * LANES].astype(jnp.float32) ** 2
                if n == 2:
                    part = jnp.where(lane < 32, part, 0.0)
                sums = jnp.where(lane == n + b, jnp.sum(part, axis=1, keepdims=True), sums)
        sums_ref[rows, :] = sums
        return carry

    lax.fori_loop(0, count, slope_step, 0)

    def curve_step(i, carry):
        rows = pl.ds(pl.multiple_of(i * tile, tile), tile)
        src = pl.ds(i * (tile // 24), tile // 24)
        matrix = d_ref[rows, :]

        def heat(curve, slope):
            slope = slope.astype(jnp.float32)
            return heat_diffusivity * curve + (release_rate * 2.0 * mixing_diffusivity) * slope**2

        pack_whole(jnp.dot(matrix, slope_ref[0], preferred_element_type=jnp.float32), out_ref, src, 0)
        curve = jnp.dot(matrix, slope_ref[1], preferred_element_type=jnp.float32)
        pack_whole(heat(curve, slope_ref[0, rows, :]), out_ref, src, 1)
        curve = jnp.dot(matrix, slope_ref[2], preferred_element_type=jnp.float32)
        pack_quarter(curve[:, :LANES], out_ref, src, 0)
        pack_quarter(heat(curve[:, LANES:], slope_ref[2, rows, :LANES]), out_ref, src, 1)
        return carry

    lax.fori_loop(0, count, curve_step, 0)


def line_terms(received, matrix):
    rows = matrix.shape[0]
    wide = (3, rows, WIDE)
    return pl.pallas_call(
        line_kernel,
        out_shape=(
            jax.ShapeDtypeStruct(received.shape, jnp.bfloat16),
            jax.ShapeDtypeStruct((rows, LANES), jnp.float32),
        ),
        in_specs=[pl.BlockSpec(memory_space=pltpu.VMEM), pl.BlockSpec(memory_space=pl.ANY)],
        scratch_shapes=[
            pltpu.VMEM(wide, jnp.bfloat16),
            pltpu.VMEM(wide, jnp.bfloat16),
            pltpu.VMEM(matrix.shape, matrix.dtype),
            pltpu.SemaphoreType.DMA,
        ],
        compiler_params=pltpu.CompilerParams(vmem_limit_bytes=LINE_VMEM_LIMIT),
        cost_estimate=pl.CostEstimate(
            flops=12 * rows * rows * WIDE, bytes_accessed=2 * rows * rows + 4 * received.size, transcendentals=0
        ),
        name="line_terms",
    )(received, matrix)


def local_kernel(
    fringe_ref, lo_ref, hi_ref, *refs
):
    fields = (refs[0:3], refs[3:6])
    slope_ref, curve_ref, speed_ref, inflow_ref, parts_ref, sums_ref = refs[6:]
    p = pl.program_id(0)
    last = pl.num_programs(0) - 1
    fringe = fringe_ref[p]
    speed = speed_ref[...]
    dissipation = None
    for f, (before, here, after) in enumerate(fields):
        x = here[0]
        upstream = jnp.where(p == 0, lo_ref[f], before[0])
        downstream = jnp.where(p == last, hi_ref[f], after[0])
        axial_slope = (downstream - upstream) * 0.5
        axial_curve = downstream - 2.0 * x + upstream
        diffusivity = (mixing_diffusivity, heat_diffusivity)[f]
        rhs = -speed * axial_slope + diffusivity * (axial_curve + curve_ref[f, 0]) + fringe * (inflow_ref[f] - x)
        if f == 0:
            depth = slope_ref[0, 0].astype(jnp.float32)
            dissipation = (2.0 * mixing_diffusivity) * (axial_slope**2 + depth**2)
            parts_ref[0, 0] = x + phase_step * rhs
        else:
            parts_ref[1, 0] = x + phase_step * (rhs + release_rate * dissipation)
    lane = lax.broadcasted_iota(jnp.int32, sums_ref.shape[1:], 1)
    sums = jnp.zeros(sums_ref.shape[1:], jnp.float32)
    for k in range(dissipation.shape[1] // ZBLK):
        part = jnp.sum(dissipation[:, k * ZBLK : (k + 1) * ZBLK], axis=1, keepdims=True)
        sums = jnp.where(lane == k, part, sums)
    sums_ref[0] = sums


def local_terms(x0, x1, lo, hi, slope, curve, speed, inflow, fringe):
    planes, rows, depth = x0.shape
    plane = lambda move: pl.BlockSpec((1, rows, depth), lambda p: (jnp.clip(p + move, 0, planes - 1), 0, 0))
    fixed = lambda shape: pl.BlockSpec(shape, lambda p: (0,) * len(shape))
    return pl.pallas_call(
        local_kernel,
        grid=(planes,),
        in_specs=[
            pl.BlockSpec(memory_space=pltpu.SMEM),
            fixed((2, rows, depth)),
            fixed((2, rows, depth)),
            plane(-1),
            plane(0),
            plane(1),
            plane(-1),
            plane(0),
            plane(1),
            pl.BlockSpec((1, 1, rows, depth), lambda p: (0, p, 0, 0)),
            pl.BlockSpec((2, 1, rows, depth), lambda p: (0, p, 0, 0)),
            fixed((rows, depth)),
            fixed((2, rows, depth)),
        ],
        out_specs=[
            pl.BlockSpec((2, 1, rows, depth), lambda p: (0, p, 0, 0)),
            pl.BlockSpec((1, rows, LANES), lambda p: (p, 0, 0)),
        ],
        out_shape=[
            jax.ShapeDtypeStruct((2, planes, rows, depth), jnp.float32),
            jax.ShapeDtypeStruct((planes, rows, LANES), jnp.float32),
        ],
        compiler_params=pltpu.CompilerParams(vmem_limit_bytes=LOCAL_VMEM_LIMIT),
        cost_estimate=pl.CostEstimate(flops=60 * x0.size, bytes_accessed=34 * x0.size, transcendentals=0),
        name="local_terms",
    )(fringe, lo, hi, x0, x0, x0, x1, x1, x1, slope, curve, speed, inflow)


def bin_sums(values, classes):
    row = classes // HB
    column = classes % HB
    bins = jnp.arange(HB, dtype=jnp.int32)[:, None]
    columns = (bins == column[None]).astype(jnp.bfloat16)
    total = 0.0
    for _ in range(3):
        term = values.astype(jnp.bfloat16)
        values = values - term.astype(jnp.float32)
        rows = jnp.where(bins == row[None], term[None], jnp.zeros((), jnp.bfloat16))
        total = total + jnp.einsum("rn,cn->rc", rows, columns, preferred_element_type=jnp.float32)
    return total


def all_sum(block, last_after):
    for axis, bits in (("gx", (1, 2)), ("wa", (1,)), ("wa", (16, 32)), ("wa", (2, 4)), ("wa", (8,))):
        if bits == (8,):
            block, last_after = lax.optimization_barrier((block, last_after))
        count = lax.axis_size(axis)
        moves = bits if len(bits) == 1 else (bits[0], bits[1], bits[0] + bits[1])
        arrived = [lax.ppermute(block, axis, [(i, i ^ move) for i in range(count)]) for move in moves]
        block = block + arrived[0]
        if len(arrived) == 3:
            block = block + (arrived[1] + arrived[2])
    return block, last_after


def body(
    mixing_ratio,
    thermal_state,
    streamwise_speed,
    implicit_derivative_matrix,
    stored_entry_slices,
    orifice_region_flag,
    arriving_slice_number,
    joint_frequency_class,
):
    matrix = implicit_derivative_matrix
    row_count, plane_count, depth_count = mixing_ratio.shape
    lines = lax.axis_size("wa")
    slab_index = lax.axis_index("gx")
    slab_count = lax.axis_size("gx")
    x0 = jnp.transpose(mixing_ratio, (1, 0, 2))
    x1 = jnp.transpose(thermal_state, (1, 0, 2))

    def exchange(packets):
        return lax.all_to_all(packets, "wa", split_axis=0, concat_axis=0, tiled=True)

    classes = jnp.transpose(joint_frequency_class, (1, 2, 0))
    packets = pack(x0, x1, classes, lines)
    packets, x0, x1 = lax.optimization_barrier((packets, x0, x1))
    received = exchange(packets)

    rounded = jnp.stack([x0, x1]).astype(jnp.bfloat16)
    depth_slope = jnp.einsum(
        "fxyj,kj->fxyk", rounded, matrix, preferred_element_type=jnp.float32
    ).astype(jnp.bfloat16)
    depth_slope, stored_entry_slices, x0, x1 = lax.optimization_barrier((depth_slope, stored_entry_slices, x0, x1))

    held_count = stored_entry_slices.shape[2]
    plane_index = arriving_slice_number[0]
    owner = plane_index // held_count
    held_plane = lax.dynamic_index_in_dim(stored_entry_slices, plane_index % held_count, 2, keepdims=False)
    database_plane = held_plane
    for move in range(1, slab_count):
        table = [(i, (i + move) % slab_count) for i in range(slab_count)]
        arrived = lax.ppermute(held_plane, "gx", table)
        database_plane = jnp.where((slab_index - move) % slab_count == owner, arrived, database_plane)
    forward = [(i, i + 1) for i in range(slab_count - 1)]
    backward = [(target, source) for source, target in forward]
    first = jnp.stack([x0[0], x1[0]])
    final = jnp.stack([x0[-1], x1[-1]])
    before = lax.ppermute(final.astype(jnp.bfloat16), "gx", forward).astype(jnp.float32)
    after = lax.ppermute(first.astype(jnp.bfloat16), "gx", backward).astype(jnp.float32)
    coflow = jnp.array([0.0, 1.0], jnp.float32)[:, None, None]
    inflow_cells = jnp.where(orifice_region_flag[None] == 1, database_plane.astype(jnp.float32), coflow)
    lo = jnp.where(slab_index == 0, inflow_cells, before)
    hi = jnp.where(slab_index == slab_count - 1, final, after)

    depth_curve = jnp.einsum("fxyj,kj->fxyk", depth_slope, matrix, preferred_element_type=jnp.float32)
    plane_numbers = (slab_index * plane_count + jnp.arange(plane_count, dtype=jnp.int32)).astype(jnp.float32)
    fringe = 1.0 / (1.0 + plane_numbers / plane_count)
    parts, local_sums = local_terms(
        x0, x1, lo, hi, depth_slope, depth_curve, streamwise_speed, inflow_cells, fringe
    )

    received, parts, local_sums = lax.optimization_barrier((received, parts, local_sums))
    returned, line_sums = line_terms(received, matrix)
    back = exchange(returned)

    per_plane = depth_count // ZBLK
    own_values = local_sums[:, :, :per_plane].transpose(0, 2, 1).reshape(-1)
    own_classes = classes.reshape(-1)
    line_values = (2.0 * mixing_diffusivity) * line_sums.reshape(lines, row_count, LANES)[..., :3]
    line_values = line_values.transpose(0, 2, 1).reshape(-1)
    codes = received[:, 6, :6, 96:120].astype(jnp.int32).reshape(lines, 2, 3, row_count)
    line_classes = (codes[:, 0] * HB + codes[:, 1]).reshape(-1)
    bins = bin_sums(
        jnp.concatenate([own_values, line_values]), jnp.concatenate([own_classes, line_classes])
    )
    summed, back = all_sum(bins, back)
    per_bin = row_count * lines * plane_count * slab_count * depth_count // (HB * HB)
    histogram = summed / per_bin

    mixture_next, temperature_next = unpack_add(parts, back)
    return (jnp.transpose(mixture_next, (1, 0, 2)), jnp.transpose(temperature_next, (1, 0, 2)), histogram)


def solution(mesh):
    in_specs = (
        P("wa", "gx", None),
        P("wa", "gx", None),
        P("wa", None),
        P(),
        P(None, "wa", "gx", None),
        P("wa", None),
        P(),
        P("wa", "gx", None),
    )
    out_specs = (P("wa", "gx", None), P("wa", "gx", None), P())
    return jax.shard_map(body, mesh=mesh, in_specs=in_specs, out_specs=out_specs, check_vma=False)
```

```python
import functools

import jax
import jax.numpy as jnp
from jax import lax
from jax.experimental import pallas as pl
from jax.experimental.pallas import tpu as pltpu
from jax.sharding import PartitionSpec as P

HB = 64
ZBLK = 128
LANES = 128
ROWS = 8

mixing_diffusivity = 0.3
heat_diffusivity = 0.4
release_rate = 0.5
phase_step = 0.2

VMEM_LIMIT = 56 * 1024 * 1024
LOCAL_VMEM_LIMIT = 16 * 1024 * 1024
LINE_VMEM_LIMIT = 56 * 1024 * 1024
UNPACK_VMEM_LIMIT = 50 * 1024 * 1024


PACK_PLANES = 6


def lane_group(shape):
    return lax.broadcasted_iota(jnp.int32, shape, len(shape) - 1) // 32


def rolled(tile, shift):
    shift = shift % LANES
    return pltpu.roll(tile, shift, 1) if shift else tile


def pack_kernel(x0_ref, x1_ref, class_ref, out_ref, wide_ref, high_ref, low_ref):
    step = pl.program_id(0)
    steps = pl.num_programs(0)
    lines = out_ref.shape[0]
    per_plane = x0_ref.shape[2] // ZBLK
    pairs = per_plane // 2
    left = per_plane * PACK_PLANES - (2 * lines - per_plane * PACK_PLANES * (steps - 1))
    first_left = per_plane * PACK_PLANES - left
    group = lane_group((ROWS, LANES))
    sublane = lax.broadcasted_iota(jnp.int32, (ROWS, LANES), 0)
    spare = (lax.broadcasted_iota(jnp.int32, (ROWS, LANES), 1) < 120) & (group == 3)

    def copy_pairs(count):
        for pair in range(count):
            p, k = pair // pairs, (pair % pairs) * 2 * ZBLK
            line = step * (PACK_PLANES * pairs) + pair
            for f, x_ref in enumerate((x0_ref, x1_ref)):
                for b in range(2):
                    for t in range(3):
                        tile = x_ref[p, ROWS * t : ROWS * t + ROWS, k + b * ZBLK : k + (b + 1) * ZBLK]
                        out_ref[line, 7 * f + 3 * b + t] = tile.astype(jnp.bfloat16)

    @pl.when(step == 0)
    def _():
        wide_ref[...] = jnp.zeros_like(wide_ref)
        for p in range(class_ref.shape[0]):
            wide_ref[p, :per_plane, : class_ref.shape[2]] = class_ref[p]
        for p in range(class_ref.shape[0]):
            codes = pltpu.roll(wide_ref[p], 96, 1)
            high = codes // HB
            high_ref[p] = high.astype(jnp.float32)
            low_ref[p] = (codes - HB * high).astype(jnp.float32)

    @pl.when(step < steps - 1)
    def _():
        copy_pairs(PACK_PLANES * pairs)

    @pl.when(step == steps - 1)
    def _():
        copy_pairs(first_left // 2)
        for m in range(left):
            block = first_left + m
            p, k = block // per_plane, (block % per_plane) * ZBLK
            plane, row = class_ref.shape[0] - PACK_PLANES + p, block % per_plane
            for q in range(4):
                line = 4 * m + q
                places = [(2 * line // per_plane, 2 * line % per_plane), (2 * line // per_plane, 2 * line % per_plane + 1)]
                places.append((plane, row))
                classes = jnp.zeros((ROWS, LANES), jnp.float32)
                for at, ref in ((0, high_ref), (3, low_ref)):
                    for b, (cp, cr) in enumerate(places):
                        classes = jnp.where(sublane == at + b, ref[cp, cr : cr + 1, :], classes)
                classes = jnp.where(spare, classes, 0.0)
                for f, x_ref in enumerate((x0_ref, x1_ref)):
                    packed = classes if f == 0 else jnp.zeros_like(classes)
                    for g in range(3):
                        tile = x_ref[p, ROWS * g : ROWS * g + ROWS, k : k + ZBLK]
                        packed = jnp.where(group == g, rolled(tile, 32 * (g - q)), packed)
                    out_ref[line, 7 * f + 6] = packed.astype(jnp.bfloat16)


def pack(x0, x1, classes, lines):
    planes, rows, depth = x0.shape
    part = pl.BlockSpec((PACK_PLANES, rows, depth), lambda i: (i, 0, 0))
    packets = (lines, 14, ROWS, LANES)
    wide = (planes, 2 * ROWS, LANES)
    return pl.pallas_call(
        pack_kernel,
        grid=(planes // PACK_PLANES,),
        in_specs=[part, part, pl.BlockSpec(classes.shape, lambda i: (0, 0, 0))],
        out_specs=pl.BlockSpec(packets, lambda i: (0, 0, 0, 0)),
        out_shape=jax.ShapeDtypeStruct(packets, jnp.bfloat16),
        scratch_shapes=[
            pltpu.VMEM(wide, jnp.int32),
            pltpu.VMEM(wide, jnp.float32),
            pltpu.VMEM(wide, jnp.float32),
        ],
        compiler_params=pltpu.CompilerParams(vmem_limit_bytes=VMEM_LIMIT),
        cost_estimate=pl.CostEstimate(flops=2 * x0.size, bytes_accessed=12 * x0.size, transcendentals=0),
        name="pack",
    )(x0, x1, classes)


def unpack_add_kernel(parts_ref, ret_ref, out0_ref, out1_ref):
    step = pl.program_id(0)
    steps = pl.num_programs(0)
    lines = ret_ref.shape[0]
    per_plane = parts_ref.shape[3] // ZBLK
    pairs = per_plane // 2
    left = per_plane * PACK_PLANES - (2 * lines - per_plane * PACK_PLANES * (steps - 1))
    first_left = per_plane * PACK_PLANES - left
    group = lane_group((ROWS, LANES))
    fields = (
        (out0_ref, phase_step * mixing_diffusivity),
        (out1_ref, phase_step),
    )

    def add_pairs(count):
        for pair in range(count):
            p, k = pair // pairs, (pair % pairs) * 2 * ZBLK
            line = step * (PACK_PLANES * pairs) + pair
            for f, (out_ref, scale) in enumerate(fields):
                for b in range(2):
                    for t in range(3):
                        at = (p, slice(ROWS * t, ROWS * t + ROWS), slice(k + b * ZBLK, k + (b + 1) * ZBLK))
                        tile = ret_ref[line, 7 * f + 3 * b + t].astype(jnp.float32)
                        out_ref[at] = parts_ref[(f, *at)] + scale * tile

    @pl.when(step < steps - 1)
    def _():
        add_pairs(PACK_PLANES * pairs)

    @pl.when(step == steps - 1)
    def _():
        add_pairs(first_left // 2)
        for m in range(left):
            block = first_left + m
            p, k = block // per_plane, (block % per_plane) * ZBLK
            for f, (out_ref, scale) in enumerate(fields):
                quarters = [ret_ref[4 * m + q, 7 * f + 6].astype(jnp.float32) for q in range(4)]
                for g in range(3):
                    tile = rolled(quarters[0], -32 * g)
                    for q in range(1, 4):
                        tile = jnp.where(group == q, rolled(quarters[q], 32 * (q - g)), tile)
                    at = (p, slice(ROWS * g, ROWS * g + ROWS), slice(k, k + ZBLK))
                    out_ref[at] = parts_ref[(f, *at)] + scale * tile


def unpack_add(parts, returned):
    _, planes, rows, depth = parts.shape
    part = pl.BlockSpec((PACK_PLANES, rows, depth), lambda i: (i, 0, 0))
    return pl.pallas_call(
        unpack_add_kernel,
        grid=(planes // PACK_PLANES,),
        in_specs=[
            pl.BlockSpec((2, PACK_PLANES, rows, depth), lambda i: (0, i, 0, 0)),
            pl.BlockSpec(returned.shape, lambda i: (0, 0, 0, 0)),
        ],
        out_specs=[part, part],
        out_shape=[jax.ShapeDtypeStruct(parts.shape[1:], jnp.float32)] * 2,
        compiler_params=pltpu.CompilerParams(vmem_limit_bytes=UNPACK_VMEM_LIMIT),
        cost_estimate=pl.CostEstimate(flops=2 * parts.size, bytes_accessed=10 * parts.size, transcendentals=0),
        name="unpack_add",
    )(parts, returned)


SOURCES = 16
WIDE = 2 * LANES
MATMUL_ROWS = 1536


def unpack_lines(r_ref, x_ref):
    def step(i, carry):
        src = pl.ds(i * SOURCES, SOURCES)
        rows = pl.ds(pl.multiple_of(i * (24 * SOURCES), 24 * SOURCES), 24 * SOURCES)
        for f in range(2):
            for b in range(2):
                tiles = r_ref[src, 7 * f + 3 * b : 7 * f + 3 * b + 3].astype(jnp.float32)
                x_ref[f, rows, b * LANES : (b + 1) * LANES] = tiles.reshape(24 * SOURCES, LANES).astype(jnp.bfloat16)
            last = r_ref[src, 7 * f + 6].astype(jnp.float32).reshape(ROWS * SOURCES, LANES)
            parts = [rolled(last, -32 * g).reshape(SOURCES, ROWS, LANES) for g in range(3)]
            tiles = jnp.stack(parts, axis=1)
            x_ref[2, rows, f * LANES : (f + 1) * LANES] = tiles.reshape(24 * SOURCES, LANES).astype(jnp.bfloat16)
        return carry

    lax.fori_loop(0, r_ref.shape[0] // SOURCES, step, 0)


def pack_whole(values, out_ref, src, f):
    for b in range(2):
        tiles = values[:, b * LANES : (b + 1) * LANES].reshape(-1, 3, ROWS, LANES)
        out_ref[src, 7 * f + 3 * b : 7 * f + 3 * b + 3] = tiles.astype(jnp.bfloat16)


def pack_quarter(values, out_ref, src, f):
    tiles = values.reshape(-1, 3, ROWS, LANES)
    group = lane_group((tiles.shape[0] * ROWS, LANES))
    packed = jnp.zeros(group.shape, jnp.float32)
    for g in range(3):
        packed = jnp.where(group == g, rolled(tiles[:, g].reshape(group.shape), 32 * g), packed)
    out_ref[src, 7 * f + 6] = packed.reshape(-1, ROWS, LANES).astype(jnp.bfloat16)


def line_kernel(r_ref, matrix_ref, out_ref, sums_ref, x_ref, slope_ref, d_ref, arrived):
    copy = pltpu.make_async_copy(matrix_ref, d_ref, arrived)
    copy.start()
    unpack_lines(r_ref, x_ref)
    copy.wait()
    tile = MATMUL_ROWS
    count = d_ref.shape[0] // tile

    def slope_step(i, carry):
        rows = pl.ds(pl.multiple_of(i * tile, tile), tile)
        lane = lax.broadcasted_iota(jnp.int32, (tile, LANES), 1)
        sums = jnp.zeros((tile, LANES), jnp.float32)
        for n in range(3):
            slope = jnp.dot(d_ref[rows, :], x_ref[n], preferred_element_type=jnp.float32).astype(jnp.bfloat16)
            slope_ref[n, rows, :] = slope
            if n == 1:
                continue
            for b in range(2) if n == 0 else range(1):
                part = slope[:, b * LANES : (b + 1) * LANES].astype(jnp.float32) ** 2
                if n == 2:
                    part = jnp.where(lane < 32, part, 0.0)
                sums = jnp.where(lane == n + b, jnp.sum(part, axis=1, keepdims=True), sums)
        sums_ref[rows, :] = sums
        return carry

    lax.fori_loop(0, count, slope_step, 0)

    def curve_step(i, carry):
        rows = pl.ds(pl.multiple_of(i * tile, tile), tile)
        src = pl.ds(i * (tile // 24), tile // 24)
        matrix = d_ref[rows, :]

        def heat(curve, slope):
            slope = slope.astype(jnp.float32)
            return heat_diffusivity * curve + (release_rate * 2.0 * mixing_diffusivity) * slope**2

        pack_whole(jnp.dot(matrix, slope_ref[0], preferred_element_type=jnp.float32), out_ref, src, 0)
        curve = jnp.dot(matrix, slope_ref[1], preferred_element_type=jnp.float32)
        pack_whole(heat(curve, slope_ref[0, rows, :]), out_ref, src, 1)
        curve = jnp.dot(matrix, slope_ref[2], preferred_element_type=jnp.float32)
        pack_quarter(curve[:, :LANES], out_ref, src, 0)
        pack_quarter(heat(curve[:, LANES:], slope_ref[2, rows, :LANES]), out_ref, src, 1)
        return carry

    lax.fori_loop(0, count, curve_step, 0)


def line_terms(received, matrix):
    rows = matrix.shape[0]
    wide = (3, rows, WIDE)
    return pl.pallas_call(
        line_kernel,
        out_shape=(
            jax.ShapeDtypeStruct(received.shape, jnp.bfloat16),
            jax.ShapeDtypeStruct((rows, LANES), jnp.float32),
        ),
        in_specs=[pl.BlockSpec(memory_space=pltpu.VMEM), pl.BlockSpec(memory_space=pl.ANY)],
        scratch_shapes=[
            pltpu.VMEM(wide, jnp.bfloat16),
            pltpu.VMEM(wide, jnp.bfloat16),
            pltpu.VMEM(matrix.shape, matrix.dtype),
            pltpu.SemaphoreType.DMA,
        ],
        compiler_params=pltpu.CompilerParams(vmem_limit_bytes=LINE_VMEM_LIMIT),
        cost_estimate=pl.CostEstimate(
            flops=12 * rows * rows * WIDE, bytes_accessed=2 * rows * rows + 4 * received.size, transcendentals=0
        ),
        name="line_terms",
    )(received, matrix)


def local_kernel(
    fringe_ref, lo_ref, hi_ref, *refs
):
    fields = (refs[0:3], refs[3:6])
    slope_ref, curve_ref, speed_ref, inflow_ref, parts_ref, sums_ref = refs[6:]
    p = pl.program_id(0)
    last = pl.num_programs(0) - 1
    fringe = fringe_ref[p]
    speed = speed_ref[...]
    dissipation = None
    for f, (before, here, after) in enumerate(fields):
        x = here[0]
        upstream = jnp.where(p == 0, lo_ref[f], before[0])
        downstream = jnp.where(p == last, hi_ref[f], after[0])
        axial_slope = (downstream - upstream) * 0.5
        axial_curve = downstream - 2.0 * x + upstream
        diffusivity = (mixing_diffusivity, heat_diffusivity)[f]
        rhs = -speed * axial_slope + diffusivity * (axial_curve + curve_ref[f, 0]) + fringe * (inflow_ref[f] - x)
        if f == 0:
            depth = slope_ref[0, 0].astype(jnp.float32)
            dissipation = (2.0 * mixing_diffusivity) * (axial_slope**2 + depth**2)
            parts_ref[0, 0] = x + phase_step * rhs
        else:
            parts_ref[1, 0] = x + phase_step * (rhs + release_rate * dissipation)
    lane = lax.broadcasted_iota(jnp.int32, sums_ref.shape[1:], 1)
    sums = jnp.zeros(sums_ref.shape[1:], jnp.float32)
    for k in range(dissipation.shape[1] // ZBLK):
        part = jnp.sum(dissipation[:, k * ZBLK : (k + 1) * ZBLK], axis=1, keepdims=True)
        sums = jnp.where(lane == k, part, sums)
    sums_ref[0] = sums


def local_terms(x0, x1, lo, hi, slope, curve, speed, inflow, fringe):
    planes, rows, depth = x0.shape
    plane = lambda move: pl.BlockSpec((1, rows, depth), lambda p: (jnp.clip(p + move, 0, planes - 1), 0, 0))
    fixed = lambda shape: pl.BlockSpec(shape, lambda p: (0,) * len(shape))
    return pl.pallas_call(
        local_kernel,
        grid=(planes,),
        in_specs=[
            pl.BlockSpec(memory_space=pltpu.SMEM),
            fixed((2, rows, depth)),
            fixed((2, rows, depth)),
            plane(-1),
            plane(0),
            plane(1),
            plane(-1),
            plane(0),
            plane(1),
            pl.BlockSpec((1, 1, rows, depth), lambda p: (0, p, 0, 0)),
            pl.BlockSpec((2, 1, rows, depth), lambda p: (0, p, 0, 0)),
            fixed((rows, depth)),
            fixed((2, rows, depth)),
        ],
        out_specs=[
            pl.BlockSpec((2, 1, rows, depth), lambda p: (0, p, 0, 0)),
            pl.BlockSpec((1, rows, LANES), lambda p: (p, 0, 0)),
        ],
        out_shape=[
            jax.ShapeDtypeStruct((2, planes, rows, depth), jnp.float32),
            jax.ShapeDtypeStruct((planes, rows, LANES), jnp.float32),
        ],
        compiler_params=pltpu.CompilerParams(vmem_limit_bytes=LOCAL_VMEM_LIMIT),
        cost_estimate=pl.CostEstimate(flops=60 * x0.size, bytes_accessed=34 * x0.size, transcendentals=0),
        name="local_terms",
    )(fringe, lo, hi, x0, x0, x0, x1, x1, x1, slope, curve, speed, inflow)


def bin_sums(values, classes):
    row = classes // HB
    column = classes % HB
    bins = jnp.arange(HB, dtype=jnp.int32)[:, None]
    columns = (bins == column[None]).astype(jnp.bfloat16)
    total = 0.0
    for _ in range(3):
        term = values.astype(jnp.bfloat16)
        values = values - term.astype(jnp.float32)
        rows = jnp.where(bins == row[None], term[None], jnp.zeros((), jnp.bfloat16))
        total = total + jnp.einsum("rn,cn->rc", rows, columns, preferred_element_type=jnp.float32)
    return total


def all_sum(block, last_after):
    def moved(axis, move):
        return lax.ppermute(block, axis, [(i, i ^ move) for i in range(lax.axis_size(axis))])

    for axis, bit in (("gx", 1), ("wa", 16)):
        arrived = [moved(axis, move) for move in (bit, 2 * bit, 3 * bit)]
        block = (block + arrived[0]) + (arrived[1] + arrived[2])
        if axis == "gx":
            block = block + moved("wa", 1)
    lines = lax.axis_size("wa")
    across = lax.ppermute(block, "wa", [(i, i ^ 8) for i in range(lines) if i % 2 == 1])
    near = jnp.where(lax.axis_index("wa") % 2 == 1, across, block)
    arrived = [lax.ppermute(block, "wa", [(i, i ^ (move + 8 * (i % 2))) for i in range(lines)]) for move in (2, 4, 6)]
    block = (near + arrived[0]) + (arrived[1] + arrived[2])
    block, last_after = lax.optimization_barrier((block, last_after))
    return block + moved("wa", 1), last_after


def body(
    mixing_ratio,
    thermal_state,
    streamwise_speed,
    implicit_derivative_matrix,
    stored_entry_slices,
    orifice_region_flag,
    arriving_slice_number,
    joint_frequency_class,
):
    matrix = implicit_derivative_matrix
    row_count, plane_count, depth_count = mixing_ratio.shape
    lines = lax.axis_size("wa")
    slab_index = lax.axis_index("gx")
    slab_count = lax.axis_size("gx")
    x0 = jnp.transpose(mixing_ratio, (1, 0, 2))
    x1 = jnp.transpose(thermal_state, (1, 0, 2))

    def exchange(packets):
        return lax.all_to_all(packets, "wa", split_axis=0, concat_axis=0, tiled=True)

    classes = jnp.transpose(joint_frequency_class, (1, 2, 0))
    packets = pack(x0, x1, classes, lines)
    packets, x0, x1 = lax.optimization_barrier((packets, x0, x1))
    received = exchange(packets)

    rounded = jnp.stack([x0, x1]).astype(jnp.bfloat16)
    depth_slope = jnp.einsum(
        "fxyj,kj->fxyk", rounded, matrix, preferred_element_type=jnp.float32
    ).astype(jnp.bfloat16)
    depth_slope, stored_entry_slices, x0, x1 = lax.optimization_barrier((depth_slope, stored_entry_slices, x0, x1))

    held_count = stored_entry_slices.shape[2]
    plane_index = arriving_slice_number[0]
    owner = plane_index // held_count
    held_plane = lax.dynamic_index_in_dim(stored_entry_slices, plane_index % held_count, 2, keepdims=False)
    database_plane = held_plane
    for move in range(1, slab_count):
        table = [(i, (i + move) % slab_count) for i in range(slab_count)]
        arrived = lax.ppermute(held_plane, "gx", table)
        database_plane = jnp.where((slab_index - move) % slab_count == owner, arrived, database_plane)
    forward = [(i, i + 1) for i in range(slab_count - 1)]
    backward = [(target, source) for source, target in forward]
    first = jnp.stack([x0[0], x1[0]])
    final = jnp.stack([x0[-1], x1[-1]])
    before = lax.ppermute(final.astype(jnp.bfloat16), "gx", forward).astype(jnp.float32)
    after = lax.ppermute(first.astype(jnp.bfloat16), "gx", backward).astype(jnp.float32)
    coflow = jnp.array([0.0, 1.0], jnp.float32)[:, None, None]
    inflow_cells = jnp.where(orifice_region_flag[None] == 1, database_plane.astype(jnp.float32), coflow)
    lo = jnp.where(slab_index == 0, inflow_cells, before)
    hi = jnp.where(slab_index == slab_count - 1, final, after)

    depth_curve = jnp.einsum("fxyj,kj->fxyk", depth_slope, matrix, preferred_element_type=jnp.float32)
    plane_numbers = (slab_index * plane_count + jnp.arange(plane_count, dtype=jnp.int32)).astype(jnp.float32)
    fringe = 1.0 / (1.0 + plane_numbers / plane_count)
    parts, local_sums = local_terms(
        x0, x1, lo, hi, depth_slope, depth_curve, streamwise_speed, inflow_cells, fringe
    )

    received, parts, local_sums = lax.optimization_barrier((received, parts, local_sums))
    returned, line_sums = line_terms(received, matrix)
    back = exchange(returned)

    per_plane = depth_count // ZBLK
    own_values = local_sums[:, :, :per_plane].transpose(0, 2, 1).reshape(-1)
    own_classes = classes.reshape(-1)
    line_values = (2.0 * mixing_diffusivity) * line_sums.reshape(lines, row_count, LANES)[..., :3]
    line_values = line_values.transpose(0, 2, 1).reshape(-1)
    codes = received[:, 6, :6, 96:120].astype(jnp.int32).reshape(lines, 2, 3, row_count)
    line_classes = (codes[:, 0] * HB + codes[:, 1]).reshape(-1)
    bins = bin_sums(
        jnp.concatenate([own_values, line_values]), jnp.concatenate([own_classes, line_classes])
    )
    per_bin = row_count * lines * plane_count * slab_count * depth_count // (HB * HB)
    histogram, back = all_sum(bins / per_bin, back)

    mixture_next, temperature_next = unpack_add(parts, back)
    return (jnp.transpose(mixture_next, (1, 0, 2)), jnp.transpose(temperature_next, (1, 0, 2)), histogram)


def solution(mesh):
    in_specs = (
        P("wa", "gx", None),
        P("wa", "gx", None),
        P("wa", None),
        P(),
        P(None, "wa", "gx", None),
        P("wa", None),
        P(),
        P("wa", "gx", None),
    )
    out_specs = (P("wa", "gx", None), P("wa", "gx", None), P())
    return jax.shard_map(body, mesh=mesh, in_specs=in_specs, out_specs=out_specs, check_vma=False)
```

```python
import functools

import jax
import jax.numpy as jnp
from jax import lax
from jax.experimental import pallas as pl
from jax.experimental.pallas import tpu as pltpu
from jax.sharding import PartitionSpec as P

HB = 64
ZBLK = 128
LANES = 128
ROWS = 8

mixing_diffusivity = 0.3
heat_diffusivity = 0.4
release_rate = 0.5
phase_step = 0.2

VMEM_LIMIT = 56 * 1024 * 1024
LOCAL_VMEM_LIMIT = 16 * 1024 * 1024
LINE_VMEM_LIMIT = 56 * 1024 * 1024
UNPACK_VMEM_LIMIT = 50 * 1024 * 1024


PACK_PLANES = 6


def lane_group(shape):
    return lax.broadcasted_iota(jnp.int32, shape, len(shape) - 1) // 32


def rolled(tile, shift):
    shift = shift % LANES
    return pltpu.roll(tile, shift, 1) if shift else tile


def pack_kernel(x0_ref, x1_ref, class_ref, out_ref, wide_ref, high_ref, low_ref):
    step = pl.program_id(0)
    steps = pl.num_programs(0)
    lines = out_ref.shape[0]
    per_plane = x0_ref.shape[2] // ZBLK
    pairs = per_plane // 2
    left = per_plane * PACK_PLANES - (2 * lines - per_plane * PACK_PLANES * (steps - 1))
    first_left = per_plane * PACK_PLANES - left
    group = lane_group((ROWS, LANES))
    sublane = lax.broadcasted_iota(jnp.int32, (ROWS, LANES), 0)
    spare = (lax.broadcasted_iota(jnp.int32, (ROWS, LANES), 1) < 120) & (group == 3)

    def copy_pairs(count):
        for pair in range(count):
            p, k = pair // pairs, (pair % pairs) * 2 * ZBLK
            line = step * (PACK_PLANES * pairs) + pair
            for f, x_ref in enumerate((x0_ref, x1_ref)):
                for b in range(2):
                    for t in range(3):
                        tile = x_ref[p, ROWS * t : ROWS * t + ROWS, k + b * ZBLK : k + (b + 1) * ZBLK]
                        out_ref[line, 7 * f + 3 * b + t] = tile.astype(jnp.bfloat16)

    @pl.when(step == 0)
    def _():
        wide_ref[...] = jnp.zeros_like(wide_ref)
        for p in range(class_ref.shape[0]):
            wide_ref[p, :per_plane, : class_ref.shape[2]] = class_ref[p]
        for p in range(class_ref.shape[0]):
            codes = pltpu.roll(wide_ref[p], 96, 1)
            high = codes // HB
            high_ref[p] = high.astype(jnp.float32)
            low_ref[p] = (codes - HB * high).astype(jnp.float32)

    @pl.when(step < steps - 1)
    def _():
        copy_pairs(PACK_PLANES * pairs)

    @pl.when(step == steps - 1)
    def _():
        copy_pairs(first_left // 2)
        for m in range(left):
            block = first_left + m
            p, k = block // per_plane, (block % per_plane) * ZBLK
            plane, row = class_ref.shape[0] - PACK_PLANES + p, block % per_plane
            for q in range(4):
                line = 4 * m + q
                places = [(2 * line // per_plane, 2 * line % per_plane), (2 * line // per_plane, 2 * line % per_plane + 1)]
                places.append((plane, row))
                classes = jnp.zeros((ROWS, LANES), jnp.float32)
                for at, ref in ((0, high_ref), (3, low_ref)):
                    for b, (cp, cr) in enumerate(places):
                        classes = jnp.where(sublane == at + b, ref[cp, cr : cr + 1, :], classes)
                classes = jnp.where(spare, classes, 0.0)
                for f, x_ref in enumerate((x0_ref, x1_ref)):
                    packed = classes if f == 0 else jnp.zeros_like(classes)
                    for g in range(3):
                        tile = x_ref[p, ROWS * g : ROWS * g + ROWS, k : k + ZBLK]
                        packed = jnp.where(group == g, rolled(tile, 32 * (g - q)), packed)
                    out_ref[line, 7 * f + 6] = packed.astype(jnp.bfloat16)


def pack(x0, x1, classes, lines):
    planes, rows, depth = x0.shape
    part = pl.BlockSpec((PACK_PLANES, rows, depth), lambda i: (i, 0, 0))
    packets = (lines, 14, ROWS, LANES)
    wide = (planes, 2 * ROWS, LANES)
    return pl.pallas_call(
        pack_kernel,
        grid=(planes // PACK_PLANES,),
        in_specs=[part, part, pl.BlockSpec(classes.shape, lambda i: (0, 0, 0))],
        out_specs=pl.BlockSpec(packets, lambda i: (0, 0, 0, 0)),
        out_shape=jax.ShapeDtypeStruct(packets, jnp.bfloat16),
        scratch_shapes=[
            pltpu.VMEM(wide, jnp.int32),
            pltpu.VMEM(wide, jnp.float32),
            pltpu.VMEM(wide, jnp.float32),
        ],
        compiler_params=pltpu.CompilerParams(vmem_limit_bytes=VMEM_LIMIT),
        cost_estimate=pl.CostEstimate(flops=2 * x0.size, bytes_accessed=12 * x0.size, transcendentals=0),
        name="pack",
    )(x0, x1, classes)


def unpack_add_kernel(parts_ref, ret_ref, out0_ref, out1_ref):
    step = pl.program_id(0)
    steps = pl.num_programs(0)
    lines = ret_ref.shape[0]
    per_plane = parts_ref.shape[3] // ZBLK
    pairs = per_plane // 2
    left = per_plane * PACK_PLANES - (2 * lines - per_plane * PACK_PLANES * (steps - 1))
    first_left = per_plane * PACK_PLANES - left
    group = lane_group((ROWS, LANES))
    fields = (
        (out0_ref, phase_step * mixing_diffusivity),
        (out1_ref, phase_step),
    )

    def add_pairs(count):
        for pair in range(count):
            p, k = pair // pairs, (pair % pairs) * 2 * ZBLK
            line = step * (PACK_PLANES * pairs) + pair
            for f, (out_ref, scale) in enumerate(fields):
                for b in range(2):
                    for t in range(3):
                        at = (p, slice(ROWS * t, ROWS * t + ROWS), slice(k + b * ZBLK, k + (b + 1) * ZBLK))
                        tile = ret_ref[line, 7 * f + 3 * b + t].astype(jnp.float32)
                        out_ref[at] = parts_ref[(f, *at)] + scale * tile

    @pl.when(step < steps - 1)
    def _():
        add_pairs(PACK_PLANES * pairs)

    @pl.when(step == steps - 1)
    def _():
        add_pairs(first_left // 2)
        for m in range(left):
            block = first_left + m
            p, k = block // per_plane, (block % per_plane) * ZBLK
            for f, (out_ref, scale) in enumerate(fields):
                quarters = [ret_ref[4 * m + q, 7 * f + 6].astype(jnp.float32) for q in range(4)]
                for g in range(3):
                    tile = rolled(quarters[0], -32 * g)
                    for q in range(1, 4):
                        tile = jnp.where(group == q, rolled(quarters[q], 32 * (q - g)), tile)
                    at = (p, slice(ROWS * g, ROWS * g + ROWS), slice(k, k + ZBLK))
                    out_ref[at] = parts_ref[(f, *at)] + scale * tile


def unpack_add(parts, returned):
    _, planes, rows, depth = parts.shape
    part = pl.BlockSpec((PACK_PLANES, rows, depth), lambda i: (i, 0, 0))
    return pl.pallas_call(
        unpack_add_kernel,
        grid=(planes // PACK_PLANES,),
        in_specs=[
            pl.BlockSpec((2, PACK_PLANES, rows, depth), lambda i: (0, i, 0, 0)),
            pl.BlockSpec(returned.shape, lambda i: (0, 0, 0, 0)),
        ],
        out_specs=[part, part],
        out_shape=[jax.ShapeDtypeStruct(parts.shape[1:], jnp.float32)] * 2,
        compiler_params=pltpu.CompilerParams(vmem_limit_bytes=UNPACK_VMEM_LIMIT),
        cost_estimate=pl.CostEstimate(flops=2 * parts.size, bytes_accessed=10 * parts.size, transcendentals=0),
        name="unpack_add",
    )(parts, returned)


SOURCES = 16
WIDE = 2 * LANES
MATMUL_ROWS = 1536


def unpack_lines(r_ref, x_ref, first, last):
    def step(i, carry):
        src = pl.ds(i * SOURCES, SOURCES)
        rows = pl.ds(pl.multiple_of(i * (24 * SOURCES), 24 * SOURCES), 24 * SOURCES)
        for f in range(2):
            for b in range(2):
                tiles = r_ref[src, 7 * f + 3 * b : 7 * f + 3 * b + 3].astype(jnp.float32)
                x_ref[f, rows, b * LANES : (b + 1) * LANES] = tiles.reshape(24 * SOURCES, LANES).astype(jnp.bfloat16)
            quarter = r_ref[src, 7 * f + 6].astype(jnp.float32).reshape(ROWS * SOURCES, LANES)
            parts = [rolled(quarter, -32 * g).reshape(SOURCES, ROWS, LANES) for g in range(3)]
            tiles = jnp.stack(parts, axis=1)
            x_ref[2, rows, f * LANES : (f + 1) * LANES] = tiles.reshape(24 * SOURCES, LANES).astype(jnp.bfloat16)
        return carry

    lax.fori_loop(first, last, step, 0)


def pack_whole(values, out_ref, src, f):
    for b in range(2):
        tiles = values[:, b * LANES : (b + 1) * LANES].reshape(-1, 3, ROWS, LANES)
        out_ref[src, 7 * f + 3 * b : 7 * f + 3 * b + 3] = tiles.astype(jnp.bfloat16)


def pack_quarter(values, out_ref, src, f):
    tiles = values.reshape(-1, 3, ROWS, LANES)
    group = lane_group((tiles.shape[0] * ROWS, LANES))
    packed = jnp.zeros(group.shape, jnp.float32)
    for g in range(3):
        packed = jnp.where(group == g, rolled(tiles[:, g].reshape(group.shape), 32 * g), packed)
    out_ref[src, 7 * f + 6] = packed.reshape(-1, ROWS, LANES).astype(jnp.bfloat16)


R_CHUNKS = 4


def line_kernel(
    lines_ref, matrix_ref, out_ref, sums_ref, x_ref, slope_ref, r_ref, d_ref, r_arrived, d_arrived
):
    sources, rows_all = r_ref.shape[0], d_ref.shape[0]
    r_step = sources // R_CHUNKS

    def r_copy(c):
        part = pl.ds(c * r_step, r_step)
        return pltpu.make_async_copy(lines_ref.at[part], r_ref.at[part], r_arrived.at[c])

    for c in range(R_CHUNKS):
        r_copy(c).start()
    d_copy = pltpu.make_async_copy(matrix_ref, d_ref, d_arrived)
    d_copy.start()
    for c in range(R_CHUNKS):
        r_copy(c).wait()
        unpack_lines(r_ref, x_ref, c * (r_step // SOURCES), (c + 1) * (r_step // SOURCES))
    d_copy.wait()
    tile = MATMUL_ROWS

    def slope_step(i, carry):
        rows = pl.ds(pl.multiple_of(i * tile, tile), tile)
        lane = lax.broadcasted_iota(jnp.int32, (tile, LANES), 1)
        sums = jnp.zeros((tile, LANES), jnp.float32)
        for n in range(3):
            slope = jnp.dot(d_ref[rows, :], x_ref[n], preferred_element_type=jnp.float32).astype(jnp.bfloat16)
            slope_ref[n, rows, :] = slope
            if n == 1:
                continue
            for b in range(2) if n == 0 else range(1):
                part = slope[:, b * LANES : (b + 1) * LANES].astype(jnp.float32) ** 2
                if n == 2:
                    part = jnp.where(lane < 32, part, 0.0)
                sums = jnp.where(lane == n + b, jnp.sum(part, axis=1, keepdims=True), sums)
        sums_ref[rows, :] = sums
        return carry

    lax.fori_loop(0, rows_all // tile, slope_step, 0)

    def curve_step(i, carry):
        rows = pl.ds(pl.multiple_of(i * tile, tile), tile)
        src = pl.ds(i * (tile // 24), tile // 24)

        def heat(curve, slope):
            slope = slope.astype(jnp.float32)
            return heat_diffusivity * curve + (release_rate * 2.0 * mixing_diffusivity) * slope**2

        pack_whole(jnp.dot(d_ref[rows, :], slope_ref[0], preferred_element_type=jnp.float32), out_ref, src, 0)
        curve = jnp.dot(d_ref[rows, :], slope_ref[1], preferred_element_type=jnp.float32)
        pack_whole(heat(curve, slope_ref[0, rows, :]), out_ref, src, 1)
        curve = jnp.dot(d_ref[rows, :], slope_ref[2], preferred_element_type=jnp.float32)
        pack_quarter(curve[:, :LANES], out_ref, src, 0)
        pack_quarter(heat(curve[:, LANES:], slope_ref[2, rows, :LANES]), out_ref, src, 1)
        return carry

    lax.fori_loop(0, rows_all // tile, curve_step, 0)


def line_terms(received, matrix):
    rows = matrix.shape[0]
    wide = (3, rows, WIDE)
    return pl.pallas_call(
        line_kernel,
        out_shape=(
            jax.ShapeDtypeStruct(received.shape, jnp.bfloat16),
            jax.ShapeDtypeStruct((rows, LANES), jnp.float32),
        ),
        in_specs=[pl.BlockSpec(memory_space=pl.ANY)] * 2,
        scratch_shapes=[
            pltpu.VMEM(wide, jnp.bfloat16),
            pltpu.VMEM(wide, jnp.bfloat16),
            pltpu.VMEM(received.shape, received.dtype),
            pltpu.VMEM(matrix.shape, matrix.dtype),
            pltpu.SemaphoreType.DMA((R_CHUNKS,)),
            pltpu.SemaphoreType.DMA,
        ],
        compiler_params=pltpu.CompilerParams(vmem_limit_bytes=LINE_VMEM_LIMIT),
        cost_estimate=pl.CostEstimate(
            flops=12 * rows * rows * WIDE, bytes_accessed=2 * rows * rows + 4 * received.size, transcendentals=0
        ),
        name="line_terms",
    )(received, matrix)


def local_kernel(
    fringe_ref, lo_ref, hi_ref, *refs
):
    fields = (refs[0:3], refs[3:6])
    slope_ref, curve_ref, speed_ref, inflow_ref, parts_ref, sums_ref = refs[6:]
    p = pl.program_id(0)
    last = pl.num_programs(0) - 1
    fringe = fringe_ref[p]
    speed = speed_ref[...]
    dissipation = None
    for f, (before, here, after) in enumerate(fields):
        x = here[0]
        upstream = jnp.where(p == 0, lo_ref[f], before[0])
        downstream = jnp.where(p == last, hi_ref[f], after[0])
        axial_slope = (downstream - upstream) * 0.5
        axial_curve = downstream - 2.0 * x + upstream
        diffusivity = (mixing_diffusivity, heat_diffusivity)[f]
        rhs = -speed * axial_slope + diffusivity * (axial_curve + curve_ref[f, 0]) + fringe * (inflow_ref[f] - x)
        if f == 0:
            depth = slope_ref[0, 0].astype(jnp.float32)
            dissipation = (2.0 * mixing_diffusivity) * (axial_slope**2 + depth**2)
            parts_ref[0, 0] = x + phase_step * rhs
        else:
            parts_ref[1, 0] = x + phase_step * (rhs + release_rate * dissipation)
    lane = lax.broadcasted_iota(jnp.int32, sums_ref.shape[1:], 1)
    sums = jnp.zeros(sums_ref.shape[1:], jnp.float32)
    for k in range(dissipation.shape[1] // ZBLK):
        part = jnp.sum(dissipation[:, k * ZBLK : (k + 1) * ZBLK], axis=1, keepdims=True)
        sums = jnp.where(lane == k, part, sums)
    sums_ref[0] = sums


def local_terms(x0, x1, lo, hi, slope, curve, speed, inflow, fringe):
    planes, rows, depth = x0.shape
    plane = lambda move: pl.BlockSpec((1, rows, depth), lambda p: (jnp.clip(p + move, 0, planes - 1), 0, 0))
    fixed = lambda shape: pl.BlockSpec(shape, lambda p: (0,) * len(shape))
    return pl.pallas_call(
        local_kernel,
        grid=(planes,),
        in_specs=[
            pl.BlockSpec(memory_space=pltpu.SMEM),
            fixed((2, rows, depth)),
            fixed((2, rows, depth)),
            plane(-1),
            plane(0),
            plane(1),
            plane(-1),
            plane(0),
            plane(1),
            pl.BlockSpec((1, 1, rows, depth), lambda p: (0, p, 0, 0)),
            pl.BlockSpec((2, 1, rows, depth), lambda p: (0, p, 0, 0)),
            fixed((rows, depth)),
            fixed((2, rows, depth)),
        ],
        out_specs=[
            pl.BlockSpec((2, 1, rows, depth), lambda p: (0, p, 0, 0)),
            pl.BlockSpec((1, rows, LANES), lambda p: (p, 0, 0)),
        ],
        out_shape=[
            jax.ShapeDtypeStruct((2, planes, rows, depth), jnp.float32),
            jax.ShapeDtypeStruct((planes, rows, LANES), jnp.float32),
        ],
        compiler_params=pltpu.CompilerParams(vmem_limit_bytes=LOCAL_VMEM_LIMIT),
        cost_estimate=pl.CostEstimate(flops=60 * x0.size, bytes_accessed=34 * x0.size, transcendentals=0),
        name="local_terms",
    )(fringe, lo, hi, x0, x0, x0, x1, x1, x1, slope, curve, speed, inflow)


def bin_sums(values, row, column):
    bins = jnp.arange(HB, dtype=jnp.int32)[:, None]
    columns = (bins == column[None]).astype(jnp.bfloat16)
    total = 0.0
    for _ in range(2):
        term = values.astype(jnp.bfloat16)
        values = values - term.astype(jnp.float32)
        rows = jnp.where(bins == row[None], term[None], jnp.zeros((), jnp.bfloat16))
        total = total + jnp.einsum("rn,cn->rc", rows, columns, preferred_element_type=jnp.float32)
    return total


def all_sum(block, last_after):
    def moved(axis, move):
        return lax.ppermute(block, axis, [(i, i ^ move) for i in range(lax.axis_size(axis))])

    for axis, bit in (("gx", 1), ("wa", 16)):
        arrived = [moved(axis, move) for move in (bit, 2 * bit, 3 * bit)]
        block = (block + arrived[0]) + (arrived[1] + arrived[2])
        if axis == "gx":
            block = block + moved("wa", 1)
    lines = lax.axis_size("wa")
    across = lax.ppermute(block, "wa", [(i, i ^ 8) for i in range(lines) if i % 2 == 1])
    near = jnp.where(lax.axis_index("wa") % 2 == 1, across, block)
    arrived = [lax.ppermute(block, "wa", [(i, i ^ (move + 8 * (i % 2))) for i in range(lines)]) for move in (2, 4, 6)]
    block = (near + arrived[0]) + (arrived[1] + arrived[2])
    block, last_after = lax.optimization_barrier((block, last_after))
    return block + moved("wa", 1), last_after


def body(
    mixing_ratio,
    thermal_state,
    streamwise_speed,
    implicit_derivative_matrix,
    stored_entry_slices,
    orifice_region_flag,
    arriving_slice_number,
    joint_frequency_class,
):
    matrix = implicit_derivative_matrix
    row_count, plane_count, depth_count = mixing_ratio.shape
    lines = lax.axis_size("wa")
    slab_index = lax.axis_index("gx")
    slab_count = lax.axis_size("gx")
    x0 = jnp.transpose(mixing_ratio, (1, 0, 2))
    x1 = jnp.transpose(thermal_state, (1, 0, 2))

    def exchange(packets):
        return lax.all_to_all(packets, "wa", split_axis=0, concat_axis=0, tiled=True)

    classes = jnp.transpose(joint_frequency_class, (1, 2, 0))
    packets = pack(x0, x1, classes, lines)
    packets, x0, x1 = lax.optimization_barrier((packets, x0, x1))
    received = exchange(packets)

    rounded = jnp.stack([x0, x1]).astype(jnp.bfloat16)
    depth_slope = jnp.einsum(
        "fxyj,kj->fxyk", rounded, matrix, preferred_element_type=jnp.float32
    ).astype(jnp.bfloat16)
    depth_slope, stored_entry_slices, x0, x1 = lax.optimization_barrier((depth_slope, stored_entry_slices, x0, x1))

    held_count = stored_entry_slices.shape[2]
    plane_index = arriving_slice_number[0]
    owner = plane_index // held_count
    held_plane = lax.dynamic_index_in_dim(stored_entry_slices, plane_index % held_count, 2, keepdims=False)
    database_plane = held_plane
    for move in range(1, slab_count):
        table = [(i, (i + move) % slab_count) for i in range(slab_count)]
        arrived = lax.ppermute(held_plane, "gx", table)
        database_plane = jnp.where((slab_index - move) % slab_count == owner, arrived, database_plane)
    forward = [(i, i + 1) for i in range(slab_count - 1)]
    backward = [(target, source) for source, target in forward]
    first = jnp.stack([x0[0], x1[0]])
    final = jnp.stack([x0[-1], x1[-1]])
    before = lax.ppermute(final.astype(jnp.bfloat16), "gx", forward).astype(jnp.float32)
    after = lax.ppermute(first.astype(jnp.bfloat16), "gx", backward).astype(jnp.float32)
    coflow = jnp.array([0.0, 1.0], jnp.float32)[:, None, None]
    inflow_cells = jnp.where(orifice_region_flag[None] == 1, database_plane.astype(jnp.float32), coflow)
    lo = jnp.where(slab_index == 0, inflow_cells, before)
    hi = jnp.where(slab_index == slab_count - 1, final, after)

    depth_curve = jnp.einsum("fxyj,kj->fxyk", depth_slope, matrix, preferred_element_type=jnp.float32)
    plane_numbers = (slab_index * plane_count + jnp.arange(plane_count, dtype=jnp.int32)).astype(jnp.float32)
    fringe = 1.0 / (1.0 + plane_numbers / plane_count)
    parts, local_sums = local_terms(
        x0, x1, lo, hi, depth_slope, depth_curve, streamwise_speed, inflow_cells, fringe
    )

    received, parts, local_sums = lax.optimization_barrier((received, parts, local_sums))
    returned, line_sums = line_terms(received, matrix)
    back = exchange(returned)

    per_plane = depth_count // ZBLK
    own_values = local_sums[:, :, :per_plane].transpose(0, 2, 1).reshape(-1)
    own_classes = classes.reshape(-1)
    line_values = (2.0 * mixing_diffusivity) * line_sums.reshape(lines, row_count, LANES)[..., :3]
    line_values = line_values.transpose(0, 2, 1).reshape(-1)
    codes = received[:, 6, :6, 96:120].astype(jnp.int32).reshape(lines, 2, 3 * row_count)
    bins = bin_sums(own_values, own_classes // HB, own_classes % HB)
    bins = bins + bin_sums(line_values, codes[:, 0].reshape(-1), codes[:, 1].reshape(-1))
    per_bin = row_count * lines * plane_count * slab_count * depth_count // (HB * HB)
    histogram, back = all_sum(bins / per_bin, back)

    mixture_next, temperature_next = unpack_add(parts, back)
    return (jnp.transpose(mixture_next, (1, 0, 2)), jnp.transpose(temperature_next, (1, 0, 2)), histogram)


def solution(mesh):
    in_specs = (
        P("wa", "gx", None),
        P("wa", "gx", None),
        P("wa", None),
        P(),
        P(None, "wa", "gx", None),
        P("wa", None),
        P(),
        P("wa", "gx", None),
    )
    out_specs = (P("wa", "gx", None), P("wa", "gx", None), P())
    return jax.shard_map(body, mesh=mesh, in_specs=in_specs, out_specs=out_specs, check_vma=False)
```

```python
import functools

import jax
import jax.numpy as jnp
from jax import lax
from jax.experimental import pallas as pl
from jax.experimental.pallas import tpu as pltpu
from jax.sharding import PartitionSpec as P

HB = 64
ZBLK = 128
LANES = 128
ROWS = 8

mixing_diffusivity = 0.3
heat_diffusivity = 0.4
release_rate = 0.5
phase_step = 0.2

VMEM_LIMIT = 56 * 1024 * 1024
LOCAL_VMEM_LIMIT = 16 * 1024 * 1024
LINE_VMEM_LIMIT = 56 * 1024 * 1024
UNPACK_VMEM_LIMIT = 50 * 1024 * 1024


PACK_PLANES = 6


def lane_group(shape):
    return lax.broadcasted_iota(jnp.int32, shape, len(shape) - 1) // 32


def rolled(tile, shift):
    shift = shift % LANES
    return pltpu.roll(tile, shift, 1) if shift else tile


def pack_kernel(x0_ref, x1_ref, class_ref, out_ref, wide_ref, high_ref, low_ref):
    step = pl.program_id(0)
    steps = pl.num_programs(0)
    lines = out_ref.shape[0]
    per_plane = x0_ref.shape[2] // ZBLK
    pairs = per_plane // 2
    left = per_plane * PACK_PLANES - (2 * lines - per_plane * PACK_PLANES * (steps - 1))
    first_left = per_plane * PACK_PLANES - left
    group = lane_group((ROWS, LANES))
    sublane = lax.broadcasted_iota(jnp.int32, (ROWS, LANES), 0)
    spare = (lax.broadcasted_iota(jnp.int32, (ROWS, LANES), 1) < 120) & (group == 3)

    def copy_pairs(count):
        for pair in range(count):
            p, k = pair // pairs, (pair % pairs) * 2 * ZBLK
            line = step * (PACK_PLANES * pairs) + pair
            for f, x_ref in enumerate((x0_ref, x1_ref)):
                for b in range(2):
                    for t in range(3):
                        tile = x_ref[p, ROWS * t : ROWS * t + ROWS, k + b * ZBLK : k + (b + 1) * ZBLK]
                        out_ref[line, 7 * f + 3 * b + t] = tile.astype(jnp.bfloat16)

    @pl.when(step == 0)
    def _():
        wide_ref[...] = jnp.zeros_like(wide_ref)
        for p in range(class_ref.shape[0]):
            wide_ref[p, :per_plane, : class_ref.shape[2]] = class_ref[p]
        for p in range(class_ref.shape[0]):
            codes = pltpu.roll(wide_ref[p], 96, 1)
            high = codes // HB
            high_ref[p] = high.astype(jnp.float32)
            low_ref[p] = (codes - HB * high).astype(jnp.float32)

    @pl.when(step < steps - 1)
    def _():
        copy_pairs(PACK_PLANES * pairs)

    @pl.when(step == steps - 1)
    def _():
        copy_pairs(first_left // 2)
        for m in range(left):
            block = first_left + m
            p, k = block // per_plane, (block % per_plane) * ZBLK
            plane, row = class_ref.shape[0] - PACK_PLANES + p, block % per_plane
            for q in range(4):
                line = 4 * m + q
                places = [(2 * line // per_plane, 2 * line % per_plane), (2 * line // per_plane, 2 * line % per_plane + 1)]
                places.append((plane, row))
                classes = jnp.zeros((ROWS, LANES), jnp.float32)
                for at, ref in ((0, high_ref), (3, low_ref)):
                    for b, (cp, cr) in enumerate(places):
                        classes = jnp.where(sublane == at + b, ref[cp, cr : cr + 1, :], classes)
                classes = jnp.where(spare, classes, 0.0)
                for f, x_ref in enumerate((x0_ref, x1_ref)):
                    packed = classes if f == 0 else jnp.zeros_like(classes)
                    for g in range(3):
                        tile = x_ref[p, ROWS * g : ROWS * g + ROWS, k : k + ZBLK]
                        packed = jnp.where(group == g, rolled(tile, 32 * (g - q)), packed)
                    out_ref[line, 7 * f + 6] = packed.astype(jnp.bfloat16)


def pack(x0, x1, classes, lines):
    planes, rows, depth = x0.shape
    part = pl.BlockSpec((PACK_PLANES, rows, depth), lambda i: (i, 0, 0))
    packets = (lines, 14, ROWS, LANES)
    wide = (planes, 2 * ROWS, LANES)
    return pl.pallas_call(
        pack_kernel,
        grid=(planes // PACK_PLANES,),
        in_specs=[part, part, pl.BlockSpec(classes.shape, lambda i: (0, 0, 0))],
        out_specs=pl.BlockSpec(packets, lambda i: (0, 0, 0, 0)),
        out_shape=jax.ShapeDtypeStruct(packets, jnp.bfloat16),
        scratch_shapes=[
            pltpu.VMEM(wide, jnp.int32),
            pltpu.VMEM(wide, jnp.float32),
            pltpu.VMEM(wide, jnp.float32),
        ],
        compiler_params=pltpu.CompilerParams(vmem_limit_bytes=VMEM_LIMIT),
        cost_estimate=pl.CostEstimate(flops=2 * x0.size, bytes_accessed=12 * x0.size, transcendentals=0),
        name="pack",
    )(x0, x1, classes)


def unpack_add_kernel(scale, parts_ref, ret_ref, out_ref):
    step = pl.program_id(0)
    steps = pl.num_programs(0)
    lines = ret_ref.shape[0]
    per_plane = parts_ref.shape[3] // ZBLK
    pairs = per_plane // 2
    left = per_plane * PACK_PLANES - (2 * lines - per_plane * PACK_PLANES * (steps - 1))
    first_left = per_plane * PACK_PLANES - left
    group = lane_group((ROWS, LANES))

    def add_pairs(count):
        for pair in range(count):
            p, k = pair // pairs, (pair % pairs) * 2 * ZBLK
            line = step * (PACK_PLANES * pairs) + pair
            for b in range(2):
                for t in range(3):
                    at = (p, slice(ROWS * t, ROWS * t + ROWS), slice(k + b * ZBLK, k + (b + 1) * ZBLK))
                    tile = ret_ref[line, 3 * b + t].astype(jnp.float32)
                    out_ref[at] = parts_ref[(0, *at)] + scale * tile

    @pl.when(step < steps - 1)
    def _():
        add_pairs(PACK_PLANES * pairs)

    @pl.when(step == steps - 1)
    def _():
        add_pairs(first_left // 2)
        for m in range(left):
            block = first_left + m
            p, k = block // per_plane, (block % per_plane) * ZBLK
            quarters = [ret_ref[4 * m + q, 6].astype(jnp.float32) for q in range(4)]
            for g in range(3):
                tile = rolled(quarters[0], -32 * g)
                for q in range(1, 4):
                    tile = jnp.where(group == q, rolled(quarters[q], 32 * (q - g)), tile)
                at = (p, slice(ROWS * g, ROWS * g + ROWS), slice(k, k + ZBLK))
                out_ref[at] = parts_ref[(0, *at)] + scale * tile


def unpack_add(parts, returned, field, scale):
    _, planes, rows, depth = parts.shape
    lines = returned.shape[0]
    return pl.pallas_call(
        functools.partial(unpack_add_kernel, scale),
        grid=(planes // PACK_PLANES,),
        in_specs=[
            pl.BlockSpec((1, PACK_PLANES, rows, depth), lambda i: (field, i, 0, 0)),
            pl.BlockSpec((lines, 7, ROWS, LANES), lambda i: (0, field, 0, 0)),
        ],
        out_specs=pl.BlockSpec((PACK_PLANES, rows, depth), lambda i: (i, 0, 0)),
        out_shape=jax.ShapeDtypeStruct(parts.shape[1:], jnp.float32),
        compiler_params=pltpu.CompilerParams(vmem_limit_bytes=UNPACK_VMEM_LIMIT),
        cost_estimate=pl.CostEstimate(flops=parts.size, bytes_accessed=5 * parts.size, transcendentals=0),
        name="unpack_add",
    )(parts, returned)


SOURCES = 16
WIDE = 2 * LANES
MATMUL_ROWS = 1536


def unpack_lines(r_ref, x_ref, first, last):
    def step(i, carry):
        src = pl.ds(i * SOURCES, SOURCES)
        rows = pl.ds(pl.multiple_of(i * (24 * SOURCES), 24 * SOURCES), 24 * SOURCES)
        for f in range(2):
            for b in range(2):
                tiles = r_ref[src, 7 * f + 3 * b : 7 * f + 3 * b + 3].astype(jnp.float32)
                x_ref[f, rows, b * LANES : (b + 1) * LANES] = tiles.reshape(24 * SOURCES, LANES).astype(jnp.bfloat16)
            quarter = r_ref[src, 7 * f + 6].astype(jnp.float32).reshape(ROWS * SOURCES, LANES)
            parts = [rolled(quarter, -32 * g).reshape(SOURCES, ROWS, LANES) for g in range(3)]
            tiles = jnp.stack(parts, axis=1)
            x_ref[2, rows, f * LANES : (f + 1) * LANES] = tiles.reshape(24 * SOURCES, LANES).astype(jnp.bfloat16)
        return carry

    lax.fori_loop(first, last, step, 0)


def pack_whole(values, out_ref, src, f):
    for b in range(2):
        tiles = values[:, b * LANES : (b + 1) * LANES].reshape(-1, 3, ROWS, LANES)
        out_ref[src, 7 * f + 3 * b : 7 * f + 3 * b + 3] = tiles.astype(jnp.bfloat16)


def pack_quarter(values, out_ref, src, f):
    tiles = values.reshape(-1, 3, ROWS, LANES)
    group = lane_group((tiles.shape[0] * ROWS, LANES))
    packed = jnp.zeros(group.shape, jnp.float32)
    for g in range(3):
        packed = jnp.where(group == g, rolled(tiles[:, g].reshape(group.shape), 32 * g), packed)
    out_ref[src, 7 * f + 6] = packed.reshape(-1, ROWS, LANES).astype(jnp.bfloat16)


R_CHUNKS = 4


def line_kernel(
    lines_ref, matrix_ref, out_ref, sums_ref, x_ref, slope_ref, r_ref, d_ref, r_arrived, d_arrived
):
    sources, rows_all = r_ref.shape[0], d_ref.shape[0]
    r_step = sources // R_CHUNKS

    def r_copy(c):
        part = pl.ds(c * r_step, r_step)
        return pltpu.make_async_copy(lines_ref.at[part], r_ref.at[part], r_arrived.at[c])

    for c in range(R_CHUNKS):
        r_copy(c).start()
    d_copy = pltpu.make_async_copy(matrix_ref, d_ref, d_arrived)
    d_copy.start()
    for c in range(R_CHUNKS):
        r_copy(c).wait()
        unpack_lines(r_ref, x_ref, c * (r_step // SOURCES), (c + 1) * (r_step // SOURCES))
    d_copy.wait()
    tile = MATMUL_ROWS

    def slope_step(i, carry):
        rows = pl.ds(pl.multiple_of(i * tile, tile), tile)
        lane = lax.broadcasted_iota(jnp.int32, (tile, LANES), 1)
        sums = jnp.zeros((tile, LANES), jnp.float32)
        for n in range(3):
            slope = jnp.dot(d_ref[rows, :], x_ref[n], preferred_element_type=jnp.float32).astype(jnp.bfloat16)
            slope_ref[n, rows, :] = slope
            if n == 1:
                continue
            for b in range(2) if n == 0 else range(1):
                part = slope[:, b * LANES : (b + 1) * LANES].astype(jnp.float32) ** 2
                if n == 2:
                    part = jnp.where(lane < 32, part, 0.0)
                sums = jnp.where(lane == n + b, jnp.sum(part, axis=1, keepdims=True), sums)
        sums_ref[rows, :] = sums
        return carry

    lax.fori_loop(0, rows_all // tile, slope_step, 0)

    def curve_step(i, carry):
        rows = pl.ds(pl.multiple_of(i * tile, tile), tile)
        src = pl.ds(i * (tile // 24), tile // 24)

        def heat(curve, slope):
            slope = slope.astype(jnp.float32)
            return heat_diffusivity * curve + (release_rate * 2.0 * mixing_diffusivity) * slope**2

        pack_whole(jnp.dot(d_ref[rows, :], slope_ref[0], preferred_element_type=jnp.float32), out_ref, src, 0)
        curve = jnp.dot(d_ref[rows, :], slope_ref[1], preferred_element_type=jnp.float32)
        pack_whole(heat(curve, slope_ref[0, rows, :]), out_ref, src, 1)
        curve = jnp.dot(d_ref[rows, :], slope_ref[2], preferred_element_type=jnp.float32)
        pack_quarter(curve[:, :LANES], out_ref, src, 0)
        pack_quarter(heat(curve[:, LANES:], slope_ref[2, rows, :LANES]), out_ref, src, 1)
        return carry

    lax.fori_loop(0, rows_all // tile, curve_step, 0)


def line_terms(received, matrix):
    rows = matrix.shape[0]
    wide = (3, rows, WIDE)
    return pl.pallas_call(
        line_kernel,
        out_shape=(
            jax.ShapeDtypeStruct(received.shape, jnp.bfloat16),
            jax.ShapeDtypeStruct((rows, LANES), jnp.float32),
        ),
        in_specs=[pl.BlockSpec(memory_space=pl.ANY)] * 2,
        scratch_shapes=[
            pltpu.VMEM(wide, jnp.bfloat16),
            pltpu.VMEM(wide, jnp.bfloat16),
            pltpu.VMEM(received.shape, received.dtype),
            pltpu.VMEM(matrix.shape, matrix.dtype),
            pltpu.SemaphoreType.DMA((R_CHUNKS,)),
            pltpu.SemaphoreType.DMA,
        ],
        compiler_params=pltpu.CompilerParams(vmem_limit_bytes=LINE_VMEM_LIMIT),
        cost_estimate=pl.CostEstimate(
            flops=12 * rows * rows * WIDE, bytes_accessed=2 * rows * rows + 4 * received.size, transcendentals=0
        ),
        name="line_terms",
    )(received, matrix)


def local_kernel(
    fringe_ref, lo_ref, hi_ref, *refs
):
    fields = (refs[0:3], refs[3:6])
    slope_ref, curve_ref, speed_ref, inflow_ref, parts_ref, sums_ref = refs[6:]
    p = pl.program_id(0)
    last = pl.num_programs(0) - 1
    fringe = fringe_ref[p]
    speed = speed_ref[...]
    dissipation = None
    for f, (before, here, after) in enumerate(fields):
        x = here[0]
        upstream = jnp.where(p == 0, lo_ref[f], before[0])
        downstream = jnp.where(p == last, hi_ref[f], after[0])
        axial_slope = (downstream - upstream) * 0.5
        axial_curve = downstream - 2.0 * x + upstream
        diffusivity = (mixing_diffusivity, heat_diffusivity)[f]
        rhs = -speed * axial_slope + diffusivity * (axial_curve + curve_ref[f, 0]) + fringe * (inflow_ref[f] - x)
        if f == 0:
            depth = slope_ref[0, 0].astype(jnp.float32)
            dissipation = (2.0 * mixing_diffusivity) * (axial_slope**2 + depth**2)
            parts_ref[0, 0] = x + phase_step * rhs
        else:
            parts_ref[1, 0] = x + phase_step * (rhs + release_rate * dissipation)
    lane = lax.broadcasted_iota(jnp.int32, sums_ref.shape[1:], 1)
    sums = jnp.zeros(sums_ref.shape[1:], jnp.float32)
    for k in range(dissipation.shape[1] // ZBLK):
        part = jnp.sum(dissipation[:, k * ZBLK : (k + 1) * ZBLK], axis=1, keepdims=True)
        sums = jnp.where(lane == k, part, sums)
    sums_ref[0] = sums


def local_terms(x0, x1, lo, hi, slope, curve, speed, inflow, fringe):
    planes, rows, depth = x0.shape
    plane = lambda move: pl.BlockSpec((1, rows, depth), lambda p: (jnp.clip(p + move, 0, planes - 1), 0, 0))
    fixed = lambda shape: pl.BlockSpec(shape, lambda p: (0,) * len(shape))
    return pl.pallas_call(
        local_kernel,
        grid=(planes,),
        in_specs=[
            pl.BlockSpec(memory_space=pltpu.SMEM),
            fixed((2, rows, depth)),
            fixed((2, rows, depth)),
            plane(-1),
            plane(0),
            plane(1),
            plane(-1),
            plane(0),
            plane(1),
            pl.BlockSpec((1, 1, rows, depth), lambda p: (0, p, 0, 0)),
            pl.BlockSpec((2, 1, rows, depth), lambda p: (0, p, 0, 0)),
            fixed((rows, depth)),
            fixed((2, rows, depth)),
        ],
        out_specs=[
            pl.BlockSpec((2, 1, rows, depth), lambda p: (0, p, 0, 0)),
            pl.BlockSpec((1, rows, LANES), lambda p: (p, 0, 0)),
        ],
        out_shape=[
            jax.ShapeDtypeStruct((2, planes, rows, depth), jnp.float32),
            jax.ShapeDtypeStruct((planes, rows, LANES), jnp.float32),
        ],
        compiler_params=pltpu.CompilerParams(vmem_limit_bytes=LOCAL_VMEM_LIMIT),
        cost_estimate=pl.CostEstimate(flops=60 * x0.size, bytes_accessed=34 * x0.size, transcendentals=0),
        name="local_terms",
    )(fringe, lo, hi, x0, x0, x0, x1, x1, x1, slope, curve, speed, inflow)


def bin_sums(values, row, column):
    bins = jnp.arange(HB, dtype=jnp.int32)[:, None]
    columns = (bins == column[None]).astype(jnp.bfloat16)
    total = 0.0
    for _ in range(2):
        term = values.astype(jnp.bfloat16)
        values = values - term.astype(jnp.float32)
        rows = jnp.where(bins == row[None], term[None], jnp.zeros((), jnp.bfloat16))
        total = total + jnp.einsum("rn,cn->rc", rows, columns, preferred_element_type=jnp.float32)
    return total


def all_sum(block, finish, back):
    def moved(axis, move):
        return lax.ppermute(block, axis, [(i, i ^ move) for i in range(lax.axis_size(axis))])

    for axis, bit in (("gx", 1), ("wa", 16)):
        arrived = [moved(axis, move) for move in (bit, 2 * bit, 3 * bit)]
        block = (block + arrived[0]) + (arrived[1] + arrived[2])
        if axis == "gx":
            block = block + moved("wa", 1)
    lines = lax.axis_size("wa")
    across = lax.ppermute(block, "wa", [(i, i ^ 8) for i in range(lines) if i % 2 == 1])
    arrived = [lax.ppermute(block, "wa", [(i, i ^ (move + 8 * (i % 2))) for i in range(lines)]) for move in (2, 4, 6)]
    mixture_next = finish(back, 0, phase_step * mixing_diffusivity)
    mixture_next, across, arrived = lax.optimization_barrier((mixture_next, across, arrived))
    near = jnp.where(lax.axis_index("wa") % 2 == 1, across, block)
    block = (near + arrived[0]) + (arrived[1] + arrived[2])
    block, back = lax.optimization_barrier((block, back))
    temperature_next = finish(back, 1, phase_step)
    return block + moved("wa", 1), mixture_next, temperature_next


def body(
    mixing_ratio,
    thermal_state,
    streamwise_speed,
    implicit_derivative_matrix,
    stored_entry_slices,
    orifice_region_flag,
    arriving_slice_number,
    joint_frequency_class,
):
    matrix = implicit_derivative_matrix
    row_count, plane_count, depth_count = mixing_ratio.shape
    lines = lax.axis_size("wa")
    slab_index = lax.axis_index("gx")
    slab_count = lax.axis_size("gx")
    x0 = jnp.transpose(mixing_ratio, (1, 0, 2))
    x1 = jnp.transpose(thermal_state, (1, 0, 2))

    def exchange(packets):
        return lax.all_to_all(packets, "wa", split_axis=0, concat_axis=0, tiled=True)

    classes = jnp.transpose(joint_frequency_class, (1, 2, 0))
    packets = pack(x0, x1, classes, lines)
    packets, x0, x1 = lax.optimization_barrier((packets, x0, x1))
    received = exchange(packets)

    rounded = jnp.stack([x0, x1]).astype(jnp.bfloat16)
    depth_slope = jnp.einsum(
        "fxyj,kj->fxyk", rounded, matrix, preferred_element_type=jnp.float32
    ).astype(jnp.bfloat16)
    depth_slope, stored_entry_slices, x0, x1 = lax.optimization_barrier((depth_slope, stored_entry_slices, x0, x1))

    held_count = stored_entry_slices.shape[2]
    plane_index = arriving_slice_number[0]
    owner = plane_index // held_count
    held_plane = lax.dynamic_index_in_dim(stored_entry_slices, plane_index % held_count, 2, keepdims=False)
    database_plane = held_plane
    for move in range(1, slab_count):
        table = [(i, (i + move) % slab_count) for i in range(slab_count)]
        arrived = lax.ppermute(held_plane, "gx", table)
        database_plane = jnp.where((slab_index - move) % slab_count == owner, arrived, database_plane)
    forward = [(i, i + 1) for i in range(slab_count - 1)]
    backward = [(target, source) for source, target in forward]
    first = jnp.stack([x0[0], x1[0]])
    final = jnp.stack([x0[-1], x1[-1]])
    before = lax.ppermute(final.astype(jnp.bfloat16), "gx", forward).astype(jnp.float32)
    after = lax.ppermute(first.astype(jnp.bfloat16), "gx", backward).astype(jnp.float32)
    coflow = jnp.array([0.0, 1.0], jnp.float32)[:, None, None]
    inflow_cells = jnp.where(orifice_region_flag[None] == 1, database_plane.astype(jnp.float32), coflow)
    lo = jnp.where(slab_index == 0, inflow_cells, before)
    hi = jnp.where(slab_index == slab_count - 1, final, after)

    depth_curve = jnp.einsum("fxyj,kj->fxyk", depth_slope, matrix, preferred_element_type=jnp.float32)
    plane_numbers = (slab_index * plane_count + jnp.arange(plane_count, dtype=jnp.int32)).astype(jnp.float32)
    fringe = 1.0 / (1.0 + plane_numbers / plane_count)
    parts, local_sums = local_terms(
        x0, x1, lo, hi, depth_slope, depth_curve, streamwise_speed, inflow_cells, fringe
    )

    received, parts, local_sums = lax.optimization_barrier((received, parts, local_sums))
    returned, line_sums = line_terms(received, matrix)
    back = exchange(returned)

    per_plane = depth_count // ZBLK
    own_values = local_sums[:, :, :per_plane].transpose(0, 2, 1).reshape(-1)
    own_classes = classes.reshape(-1)
    line_values = (2.0 * mixing_diffusivity) * line_sums.reshape(lines, row_count, LANES)[..., :3]
    line_values = line_values.transpose(0, 2, 1).reshape(-1)
    codes = received[:, 6, :6, 96:120].astype(jnp.int32).reshape(lines, 2, 3 * row_count)
    bins = bin_sums(own_values, own_classes // HB, own_classes % HB)
    bins = bins + bin_sums(line_values, codes[:, 0].reshape(-1), codes[:, 1].reshape(-1))
    per_bin = row_count * lines * plane_count * slab_count * depth_count // (HB * HB)
    finish = functools.partial(unpack_add, parts)
    histogram, mixture_next, temperature_next = all_sum(bins / per_bin, finish, back)

    return (jnp.transpose(mixture_next, (1, 0, 2)), jnp.transpose(temperature_next, (1, 0, 2)), histogram)


def solution(mesh):
    in_specs = (
        P("wa", "gx", None),
        P("wa", "gx", None),
        P("wa", None),
        P(),
        P(None, "wa", "gx", None),
        P("wa", None),
        P(),
        P("wa", "gx", None),
    )
    out_specs = (P("wa", "gx", None), P("wa", "gx", None), P())
    return jax.shard_map(body, mesh=mesh, in_specs=in_specs, out_specs=out_specs, check_vma=False)
```
